512 devices in a mesh: curve: 128 (over y, z, core), oct: 4 (over x).
Axes of the slice: x: 4, y: 4, z: 16, core: 2. Of those that a mesh axis runs over, the one named last changes fastest.
Arguments:
- leaf_mult: bfloat16 [152, 1048576], P(None, ('curve', 'oct')), may hold values from -6 to 6
- occupancy: int32 [1048576], P(('curve', 'oct')), may hold values from 0 to 64, as said below
- ghost_rows: int32 [6, 131072], P(None, ('curve', 'oct')), may hold values from 0 to 2047
- m2l_list: int32 [32, 1048576], P(None, ('curve', 'oct')), may hold values from 0 to 3584
- par_code: int32 [131072], P(('curve', 'oct')), may hold values from 0 to 7
- coarse_of: int32 [131072], P(('curve', 'oct')), may hold values from 0 to 63, as said below
- coarse_list: int32 [32, 64], replicated, may hold values from 0 to 64
- m2m: bfloat16 [8, 152, 152], replicated, may hold values from -0.15625 to 0.15625
- coarse_up: bfloat16 [8, 152, 152], replicated, may hold values from -0.009765625 to 0.009765625
- m2l: bfloat16 [32, 152, 152], replicated, may hold values from -0.078125 to 0.078125
- l2l: bfloat16 [8, 152, 152], replicated, may hold values from -0.5 to 0.5
Outputs:
- leaf_local: bfloat16 [152, 1048576], P(None, ('curve', 'oct'))
The draws below stay inside these ranges and needn't reach their ends.
Inputs may be any that keep to these rules, and one draw needn't show every extreme that they name: `occupancy`: on each device the slots with sources come first and the rest are empty; the number of occupied slots differs from device to device and some device is full. `m2l_list`: entries 2048 + k * 256 + t name column t of ghost block k; the largest value names the zero column. `coarse_of`: never falls by more than two along the parents. `coarse_list`: the value 64 means no partner.
All inputs are finite; a program needn't handle non-finite values.
Results may differ from the reference program's by a relative error of at most 0.01.
Values may be sent and summed in bfloat16 or wider, within the bound.
No kernel may reach another device: no remote copies, remote signals or barrier semaphores. Data moves between devices by JAX's collectives and lax.ppermute only.
A program may use at most 64 MiB of HBM per device.

```python
import jax
import jax.numpy as jnp
from jax import lax

P_SIZE = 152
OFFSETS = 32
REACH = 3
COARSE = 64
BOX = 2048
GHOST = 256
BOXES = 1048576
PARENTS = 131072
N_CURVE = 128
N_OCT = 4


def draw_occupancy(key, part):
    key = jax.random.fold_in(key, 11)
    key_living, key_filled, key_counts = jax.random.split(key, 3)
    devices = BOXES // BOX
    living = jax.random.randint(key_living, (devices,), BOX // 4, BOX + 1)
    filled = jax.random.randint(key_filled, (), 0, devices)
    living = jnp.where(jnp.arange(devices) == filled, BOX, living)
    counts = jax.random.randint(key_counts, (devices, BOX), 1, 65)
    slotted = jnp.arange(BOX)[None, :]
    return jnp.where(slotted < living[:, None], counts, 0).reshape(-1).astype(jnp.int32)


def draw_coarse_of(key, part):
    key = jax.random.fold_in(key, 23)
    base_index = jnp.arange(PARENTS, dtype=jnp.int32) * COARSE // PARENTS
    jitter = jax.random.randint(key, (PARENTS,), -1, 2)
    placed = jnp.clip(base_index + jitter, 0, COARSE - 1)
    placed = placed.at[0].set(0).at[PARENTS - 1].set(COARSE - 1)
    return placed.astype(jnp.int32)


def touch_ends(array, stream_key, smallest, top_value):
    longest = array.shape.index(max(array.shape))
    spots = []
    for shift in (0, 1):
        where = [jax.random.randint(jax.random.fold_in(stream_key, axis), (), 0, length) for axis, length in enumerate(array.shape)]
        where[longest] = (where[longest] + shift) % array.shape[longest]
        spots.append(tuple(where))
    return array.at[spots[0]].set(smallest).at[spots[1]].set(top_value)


def steps_of(key, extent, pieces, least, largest):
    loudness = 1.0
    for dim, parts in pieces:
        steps = jax.random.uniform(jax.random.fold_in(jax.random.fold_in(key, 6), dim), (parts,), jnp.float32, least / len(pieces), largest / len(pieces))
        loudness = loudness * jnp.repeat(jnp.exp(steps), extent[dim] // parts).reshape((-1,) + (1,) * (len(extent) - 1 - dim))
    return loudness


def scatter_about(stream_key, shape, scale, reach, cuts=(), kind=jnp.bfloat16):
    drawn = jax.random.normal(stream_key, shape, jnp.float32) * scale
    if len(cuts) > 0:
        drawn = steps_of(stream_key, shape, cuts, -0.22, 0.18) * drawn
    return jnp.clip(drawn, min=-reach, max=reach).astype(kind)


def setup_inputs(seed: int = 0) -> dict:
    arg_keys = jax.random.split(jax.random.key(seed), 12)
    leaf_mult = scatter_about(arg_keys[0], (P_SIZE, BOXES), 1.0, 6.0, ((1, 512),))
    occupancy = draw_occupancy(jax.random.fold_in(arg_keys[11], 71), 0)
    ghost_rows = touch_ends(jax.random.randint(arg_keys[2], (2 * REACH, GHOST * N_CURVE * N_OCT), 0, BOX), jax.random.fold_in(arg_keys[2], 1), 0, BOX - 1).astype(jnp.int32)
    m2l_list = touch_ends(jax.random.randint(arg_keys[3], (OFFSETS, BOXES), 0, BOX + 2 * REACH * GHOST + 1), jax.random.fold_in(arg_keys[3], 1), 0, BOX + 2 * REACH * GHOST).astype(jnp.int32)
    par_code = touch_ends(jax.random.randint(arg_keys[4], (PARENTS,), 0, 8), jax.random.fold_in(arg_keys[4], 1), 0, 7).astype(jnp.int32)
    coarse_of = draw_coarse_of(jax.random.fold_in(arg_keys[11], 71), 0)
    coarse_list = touch_ends(jax.random.randint(arg_keys[6], (OFFSETS, COARSE), 0, COARSE + 1), jax.random.fold_in(arg_keys[6], 1), 0, COARSE).astype(jnp.int32)
    m2m = scatter_about(arg_keys[7], (8, P_SIZE, P_SIZE), (8 * P_SIZE) ** -0.5, 0.15625)
    coarse_up = scatter_about(arg_keys[8], (8, P_SIZE, P_SIZE), (P_SIZE * PARENTS // COARSE) ** -0.5, 0.009765625)
    m2l = scatter_about(arg_keys[9], (OFFSETS, P_SIZE, P_SIZE), (OFFSETS * P_SIZE) ** -0.5, 0.078125)
    l2l = scatter_about(arg_keys[10], (8, P_SIZE, P_SIZE), P_SIZE ** -0.5, 0.5)
    return dict(leaf_mult=leaf_mult, occupancy=occupancy, ghost_rows=ghost_rows, m2l_list=m2l_list, par_code=par_code, coarse_of=coarse_of, coarse_list=coarse_list, m2m=m2m, coarse_up=coarse_up, m2l=m2l, l2l=l2l)


def reference(leaf_mult, occupancy, ghost_rows, m2l_list, par_code, coarse_of, coarse_list, m2m, coarse_up, m2l, l2l):
    devices = N_CURVE * N_OCT
    scaled = occupancy.astype(jnp.float32) * 0.03125
    charged = (leaf_mult.astype(jnp.float32) * scaled[None, :]).astype(jnp.bfloat16)
    stride_list = [stride for stride in range(-REACH, REACH + 1) if stride != 0]
    anchor = (jnp.arange(devices, dtype=jnp.int32) * BOX)[:, None]
    blocks = []
    for position, stride in enumerate(stride_list):
        chosen = ghost_rows[position].reshape(devices, GHOST) + anchor
        shipped = jnp.take(charged, chosen.reshape(-1), axis=1).reshape(P_SIZE, N_CURVE, N_OCT, GHOST)
        vacant = jnp.zeros((P_SIZE, abs(stride), N_OCT, GHOST), jnp.bfloat16)
        if stride > 0:
            shifted = jnp.concatenate([vacant, shipped[:, :N_CURVE - stride]], axis=1)
        else:
            shifted = jnp.concatenate([shipped[:, -stride:], vacant], axis=1)
        blocks.append(shifted)
    owned_cols = charged.reshape(P_SIZE, N_CURVE, N_OCT, BOX)
    zero_col = jnp.zeros((P_SIZE, N_CURVE, N_OCT, 1), jnp.bfloat16)
    extended = jnp.concatenate([owned_cols] + blocks + [zero_col], axis=3)
    span_cols = BOX + 2 * REACH * GHOST + 1
    flattened = extended.reshape(P_SIZE, devices * span_cols)
    offsets_base = (jnp.arange(devices, dtype=jnp.int32) * span_cols)[:, None]

    def far_step(running, operands):
        operator, column = operands
        where_from = (column.reshape(devices, BOX) + offsets_base).reshape(-1)
        gathered = jnp.take(flattened, where_from, axis=1)
        return running + jnp.dot(operator, gathered, preferred_element_type=jnp.float32), None

    leaf_far, _ = lax.scan(far_step, jnp.zeros((P_SIZE, BOXES), jnp.float32), (m2l, m2l_list))

    children = charged.reshape(P_SIZE, PARENTS, 8).astype(jnp.float32)
    parent_mult = jnp.einsum("kpq,qbk->pb", m2m.astype(jnp.float32), children).astype(jnp.bfloat16)
    codes = jnp.arange(8, dtype=jnp.int32)
    picked = par_code[None, :] == codes[:, None]
    stacked = jnp.where(picked[:, None, :], parent_mult[None].astype(jnp.float32), jnp.float32(0.0))
    lifted = jnp.einsum("kpq,kqb->pb", coarse_up.astype(jnp.float32), stacked)
    coarse_mult = jax.ops.segment_sum(lifted.T, coarse_of, num_segments=COARSE).T.astype(jnp.bfloat16)
    coarse_ext = jnp.concatenate([coarse_mult, jnp.zeros((P_SIZE, 1), jnp.bfloat16)], axis=1)

    def coarse_step(running, operands):
        operator, column = operands
        gathered = jnp.take(coarse_ext, column, axis=1)
        return running + jnp.dot(operator, gathered, preferred_element_type=jnp.float32), None

    coarse_acc, _ = lax.scan(coarse_step, jnp.zeros((P_SIZE, COARSE), jnp.float32), (m2l, coarse_list))
    coarse_local = coarse_acc.astype(jnp.bfloat16)
    pulled = jnp.take(coarse_local, coarse_of, axis=1).astype(jnp.float32)
    stacked_down = jnp.where(picked[:, None, :], pulled[None], jnp.float32(0.0))
    parent_local = jnp.einsum("kpq,kqb->pb", l2l.astype(jnp.float32), stacked_down).astype(jnp.bfloat16)
    descended = jnp.einsum("kpq,qb->pbk", l2l.astype(jnp.float32), parent_local.astype(jnp.float32)).reshape(P_SIZE, BOXES)
    result = jnp.where((occupancy > 0)[None, :], leaf_far + descended, jnp.float32(0.0))
    return result.astype(jnp.bfloat16)
```

```python
import jax
import jax.numpy as jnp
from jax import lax
from jax.experimental import pallas as pl
from jax.experimental.pallas import tpu as pltpu
from jax.sharding import Mesh, PartitionSpec as P

REACH = 3
COARSE = 64
LANES = 128
WIDE = 256
PAD = 8
TILE = 256
CURVE = ("y", "z", "core")
NT = (((1,), (1,)), ((), ()))
BF16 = jnp.bfloat16
F32 = jnp.float32

VMEM = pl.BlockSpec(memory_space=pltpu.VMEM)
SMEM = pl.BlockSpec(memory_space=pltpu.SMEM)
HBM = pl.BlockSpec(memory_space=pltpu.HBM)


def params(mib):
    return pltpu.CompilerParams(vmem_limit_bytes=mib * 2**20)


def cost(flops, bytes_accessed):
    return pl.CostEstimate(flops=flops, bytes_accessed=bytes_accessed, transcendentals=0)


def passed_along(block, axis, distance):
    devices = range(lax.axis_size(axis))
    route = [(i - distance, i) for i in devices if i - distance in devices]
    return lax.ppermute(block, axis, route)


def split_rows(columns):
    points, n = columns.shape
    first = columns[:LANES].T
    rest = jnp.concatenate([columns[LANES:], jnp.zeros((WIDE - points, n), F32)], axis=0)
    return first, rest.T


def picked_rows(load, count):
    sublane = lax.broadcasted_iota(jnp.int32, (8, LANES), 0)
    past = [sublane >= 2 * k for k in range(4)]
    for group in range(count // 4):
        merged = load(4 * group, 0)
        for k in range(1, 4):
            merged = jnp.where(past[k], load(4 * group + k, k), merged)
        yield group, merged


def local_kernel(
    leaf_hbm, occ_hbm, rows_hbm, code_hbm, group_hbm, m2m_hbm, up_hbm, table_ref, partial_ref, *rest
):
    packets = rest[: 2 * REACH]
    padded, chosen, leaf_ref, occ_ref, rows_ref, code_ref, group_ref, m2m_ref, up_ref, sems = rest[
        2 * REACH :
    ]
    copies = [
        pltpu.make_async_copy(source, target, sems.at[n])
        for n, (source, target) in enumerate(
            [
                (occ_hbm, occ_ref),
                (leaf_hbm, leaf_ref),
                (rows_hbm, rows_ref),
                (code_hbm, code_ref),
                (group_hbm, group_ref),
                (m2m_hbm, m2m_ref),
                (up_hbm, up_ref),
            ]
        )
    ]
    for copy in copies:
        copy.start()
    points, slots = leaf_ref.shape
    parents = code_ref.shape[1]
    ghost = rows_ref.shape[1]
    padded[pl.ds(0, PAD), :] = jnp.zeros((PAD, LANES), F32)
    padded[pl.ds(PAD + 2 * slots, PAD), :] = jnp.zeros((PAD, LANES), F32)
    copies[0].wait()
    copies[1].wait()
    for c in range(0, slots, TILE):
        scale = occ_ref[:, c : c + TILE].astype(F32) * 0.03125
        charged = (leaf_ref[:, c : c + TILE].astype(F32) * scale).astype(BF16).astype(F32)
        first, second = split_rows(charged)
        padded[pl.ds(PAD + 2 * c, TILE, stride=2), :] = first
        padded[pl.ds(PAD + 2 * c + 1, TILE, stride=2), :] = second
        table_ref[pl.ds(c, TILE), :] = first
        table_ref[pl.ds(slots + c, TILE), :] = second
    copies[2].wait()

    def one_offset(q, carry):
        base = pl.multiple_of(q * 2 * ghost, 2 * ghost)
        for group, rows in picked_rows(
            lambda n, k: padded[pl.ds(rows_ref[q, n] * 2 + (PAD - 2 * k), 8), :], ghost
        ):
            chosen[pl.ds(base + 8 * group, 8), :] = rows
        return carry

    lax.fori_loop(0, 2 * REACH, one_offset, 0)
    for q in range(2 * REACH):
        first = chosen[pl.ds(q * 2 * ghost, ghost, stride=2), :].T
        second = chosen[pl.ds(q * 2 * ghost + 1, ghost, stride=2), :].T
        packets[q][...] = jnp.concatenate([first, second[: points - LANES]], axis=0).astype(BF16)
    for copy in copies[3:]:
        copy.wait()
    parent = jnp.zeros((points, parents), F32)
    for k in range(8):
        first = table_ref[pl.ds(k, parents, stride=8), :]
        second = table_ref[pl.ds(slots + k, parents, stride=8), :]
        child = jnp.concatenate([first, second], axis=1).astype(BF16)[:, :points]
        parent += lax.dot_general(m2m_ref[k], child, NT, preferred_element_type=F32)
    parent = parent.astype(BF16).astype(F32)
    code = code_ref[...]
    lifted = jnp.zeros((points, parents), F32)
    for k in range(8):
        mine = jnp.where(code == k, parent, 0.0).astype(BF16)
        lifted += jnp.dot(up_ref[k], mine, preferred_element_type=F32)
    high = lifted.astype(BF16)
    low = (lifted - high.astype(F32)).astype(BF16)
    group = lax.broadcasted_iota(jnp.int32, (2 * COARSE, parents), 0)
    left = jnp.where(group == group_ref[...], 1.0, 0.0).astype(BF16)
    right = jnp.where(group - COARSE == group_ref[...], 1.0, 0.0).astype(BF16)

    def summed(member):
        return lax.dot_general(high, member, NT, preferred_element_type=F32) + lax.dot_general(
            low, member, NT, preferred_element_type=F32
        )

    top = partial_ref.shape[0]
    below = jnp.concatenate(
        [summed(right)[top:], jnp.zeros((2 * top - points, 2 * COARSE), F32)], axis=0
    )
    partial_ref[...] = summed(left)[:top] + below


def prepare_kernel(near_ref, m2l_ref, weight_ref, sum_ref):
    offsets, points, _ = m2l_ref.shape
    sum_ref[...] = jnp.sum(near_ref[...], axis=0)

    def one_operator(r, carry):
        operator = m2l_ref[r].astype(F32)
        wide = jnp.concatenate([operator, jnp.zeros((WIDE - points, points), F32)], axis=0)
        first = wide[:, :LANES].T
        second = jnp.concatenate(
            [wide[:, LANES:], jnp.zeros((WIDE, WIDE - points), F32)], axis=1
        ).T
        base = pl.multiple_of(r * WIDE, WIDE)
        weight_ref[pl.ds(base, LANES), :] = first.astype(BF16)
        weight_ref[pl.ds(base + LANES, LANES), :] = second.astype(BF16)
        return carry

    lax.fori_loop(0, offsets, one_operator, 0)


def far_kernel(index_hbm, table_ref, weight_ref, *rest):
    ghosts, (far_ref, table, index, even, odd, index_sem) = rest[: 2 * REACH], rest[2 * REACH :]
    points, ghost = ghosts[0].shape
    slots = far_ref.shape[0]
    tiles = slots // TILE
    pairs = weight_ref.shape[0] // (2 * WIDE)
    chunks = index_sem.shape[0]
    chunk = index.shape[0] // chunks
    boxes = table.reshape(table.shape[0] // 8, 8, LANES)

    def index_copy(n):
        at = pl.ds(pl.multiple_of(n * chunk, chunk), chunk)
        return pltpu.make_async_copy(index_hbm.at[at], index.at[at], index_sem.at[n])

    for n in range(chunks):
        index_copy(n).start()

    def spread(first_box, first, second):
        for sublane in range(8):
            at = pl.ds(first_box * 8 + sublane, TILE, stride=8)
            table[at, :] = second if sublane % 2 else first

    def own_tile(n, carry):
        at = pl.multiple_of(n * TILE, TILE)
        spread(at, table_ref[pl.ds(at, TILE), :], table_ref[pl.ds(slots + at, TILE), :])
        return carry

    lax.fori_loop(0, tiles, own_tile, 0)
    for q in range(2 * REACH):
        spread(slots + q * ghost, *split_rows(ghosts[q][...].astype(F32)))
    table[pl.ds(8 * (slots + 2 * REACH * ghost), 8), :] = jnp.zeros((8, LANES), F32)
    far_ref[...] = jnp.zeros_like(far_ref)
    index_copy(0).wait()

    def gather(step, block):
        pair = step // tiles
        base = (
            (pair // 4) * (8 * slots)
            + lax.rem(step, tiles) * (8 * TILE)
            + lax.rem(pair, 4) * (2 * LANES)
        )
        for half in range(2):
            for j in range(TILE // LANES):
                spot = base + half * LANES + j * 8 * LANES
                for group, rows in picked_rows(lambda n, k: boxes[index[spot + n]], LANES):
                    block[pl.ds(half * 2 * TILE + j * 2 * LANES + 8 * group, 8), :] = rows

    def multiply(step, block):
        pair = step // tiles
        parts = [
            block[pl.ds(half * 2 * TILE + part, TILE, stride=2), :].astype(BF16)
            for half in range(2)
            for part in range(2)
        ]
        weights = weight_ref[pl.ds(pl.multiple_of(pair * 2 * WIDE, 2 * WIDE), 2 * WIDE), :]
        rows = pl.ds(pl.multiple_of(lax.rem(step, tiles) * TILE, TILE), TILE)
        far_ref[rows, :] += jnp.dot(
            jnp.concatenate(parts, axis=1), weights, preferred_element_type=F32
        )

    steps = pairs * tiles
    per_chunk = steps // chunks // 2
    gather(0, even)

    def two_steps(n, carry):
        @pl.when((lax.rem(n + 1, per_chunk) == 0) & (n + 1 < steps // 2))
        def _():
            index_copy((n + 1) // per_chunk).wait()

        gather(2 * n + 1, odd)
        multiply(2 * n, even)
        gather(jnp.minimum(2 * n + 2, steps - 1), even)
        multiply(2 * n + 1, odd)
        return carry

    lax.fori_loop(0, steps // 2, two_steps, 0)


def downward_kernel(
    coarse_ref, far_ref, occ_ref, code_ref, group_ref, list_ref, m2l_ref, l2l_ref, out_ref, first_ref, second_ref
):
    offsets, points, _ = m2l_ref.shape
    parents = code_ref.shape[1]
    slots = out_ref.shape[1]
    top = coarse_ref.shape[1]
    coarse = jnp.sum(coarse_ref[...], axis=0).astype(BF16)
    wanted = list_ref[...]
    wanted = jnp.where(wanted == COARSE, 4 * COARSE, wanted)
    row = lax.broadcasted_iota(jnp.int32, (2 * COARSE, wanted.shape[1]), 0)
    left = jnp.where(row == wanted, 1.0, 0.0).astype(BF16)
    right = jnp.where(row - COARSE == wanted, 1.0, 0.0).astype(BF16)
    upper = jnp.dot(coarse, left, preferred_element_type=F32)
    lower = jnp.dot(coarse, right, preferred_element_type=F32)
    partners = jnp.concatenate([upper, lower[: points - top]], axis=0).astype(BF16)
    sums = [jnp.zeros((points, 2 * COARSE), F32) for _ in range(2)]
    for r in range(offsets):
        at = (r // 2) * 2 * COARSE
        sums[r % 2] += jnp.dot(
            m2l_ref[r], partners[:, at : at + 2 * COARSE], preferred_element_type=F32
        )
    local = (sums[0][:, :COARSE] + sums[1][:, COARSE:]).astype(BF16)
    member = lax.broadcasted_iota(jnp.int32, (COARSE, parents), 0) == group_ref[...]
    pulled = jnp.dot(local, jnp.where(member, 1.0, 0.0).astype(BF16), preferred_element_type=F32)
    code = code_ref[...]
    parent = jnp.zeros((points, parents), F32)
    for k in range(8):
        mine = jnp.where(code == k, pulled, 0.0).astype(BF16)
        parent += jnp.dot(l2l_ref[k], mine, preferred_element_type=F32)
    parent = parent.astype(BF16).astype(F32)
    first, second = split_rows(parent)
    parent_rows = jnp.concatenate([first, second], axis=1).astype(BF16)[:, :points]
    for k in range(8):
        lowered = lax.dot_general(parent_rows, l2l_ref[k], NT, preferred_element_type=F32)
        lowered = jnp.concatenate([lowered, jnp.zeros((parents, WIDE - points), F32)], axis=1)
        first_ref[pl.ds(k, parents, stride=8), :] = lowered[:, :LANES]
        second_ref[pl.ds(k, parents, stride=8), :] = lowered[:, LANES:]
    for c in range(0, slots, TILE):
        rows = pl.ds(c, TILE)
        first = (far_ref[rows, :LANES] + first_ref[rows, :]).T
        second = (far_ref[rows, LANES:] + second_ref[rows, :]).T
        whole = jnp.concatenate([first, second[: points - LANES]], axis=0)
        live = occ_ref[:, c : c + TILE] > 0
        out_ref[:, c : c + TILE] = jnp.where(live, whole, 0.0).astype(BF16)


def shards(
    leaf_mult,
    occupancy,
    ghost_rows,
    m2l_list,
    par_code,
    coarse_of,
    coarse_list,
    m2m,
    coarse_up,
    m2l,
    l2l,
):
    points, slots = leaf_mult.shape
    parents = slots // 8
    offsets = m2l.shape[0]
    ghost = ghost_rows.shape[1]
    top = 80
    shape = jax.ShapeDtypeStruct
    occ = occupancy.reshape(1, slots)
    code = par_code.reshape(1, parents)
    group = coarse_of.reshape(1, parents)

    table, partial, *packets = pl.pallas_call(
        local_kernel,
        out_shape=[shape((2 * slots, LANES), F32), shape((top, 2 * COARSE), F32)]
        + [shape((points, ghost), BF16)] * (2 * REACH),
        in_specs=[HBM] * 7,
        out_specs=[VMEM] * (2 + 2 * REACH),
        scratch_shapes=[
            pltpu.VMEM((2 * slots + 2 * PAD, LANES), F32),
            pltpu.VMEM((4 * REACH * ghost, LANES), F32),
            pltpu.VMEM(leaf_mult.shape, BF16),
            pltpu.VMEM(occ.shape, jnp.int32),
            pltpu.SMEM(ghost_rows.shape, jnp.int32),
            pltpu.VMEM(code.shape, jnp.int32),
            pltpu.VMEM(group.shape, jnp.int32),
            pltpu.VMEM(m2m.shape, BF16),
            pltpu.VMEM(coarse_up.shape, BF16),
            pltpu.SemaphoreType.DMA((7,)),
        ],
        compiler_params=params(60),
        cost_estimate=cost(10**9, 2**22),
        name="local",
    )(leaf_mult, occ, ghost_rows, code, group, m2m, coarse_up)
    near = lax.all_gather(partial, ("y", "oct"))
    stride_list = [stride for stride in range(-REACH, REACH + 1) if stride != 0]
    ghosts = [passed_along(packets[n], CURVE, stride) for n, stride in enumerate(stride_list)]
    weights, near_sum = pl.pallas_call(
        prepare_kernel,
        out_shape=[shape((offsets * WIDE, WIDE), BF16), shape(partial.shape, F32)],
        in_specs=[VMEM, VMEM],
        out_specs=[VMEM, VMEM],
        compiler_params=params(24),
        cost_estimate=cost(10**9, 2**23),
        name="prepare",
    )(near, m2l)
    everywhere = lax.all_gather(near_sum, ("z", "core"))
    index = m2l_list.reshape(offsets // 8, 8, slots // LANES, LANES)
    index = index.transpose(0, 2, 1, 3).reshape(-1)
    far = pl.pallas_call(
        far_kernel,
        out_shape=shape((slots, WIDE), F32),
        in_specs=[HBM] + [VMEM] * (2 + 2 * REACH),
        out_specs=VMEM,
        scratch_shapes=[
            pltpu.VMEM((8 * (slots + 2 * REACH * ghost + 1), LANES), F32),
            pltpu.SMEM((offsets * slots,), jnp.int32),
            pltpu.VMEM((4 * TILE, LANES), F32),
            pltpu.VMEM((4 * TILE, LANES), F32),
            pltpu.SemaphoreType.DMA((4,)),
        ],
        compiler_params=params(40),
        cost_estimate=cost(4 * 10**10, 2**24),
        name="far",
    )(index, table, weights, *ghosts)
    return pl.pallas_call(
        downward_kernel,
        out_shape=shape((points, slots), BF16),
        in_specs=[VMEM] * 8,
        out_specs=VMEM,
        scratch_shapes=[pltpu.VMEM((slots, LANES), F32)] * 2,
        compiler_params=params(32),
        cost_estimate=cost(10**9, 2**23),
        name="downward",
    )(everywhere, far, occ, code, group, coarse_list.reshape(1, -1), m2l, l2l)


def solution(mesh):
    along, across = mesh.devices.shape
    rows = 4 if along % 32 == 0 else 1
    torus = Mesh(
        mesh.devices.reshape(rows, along // rows // 2, 2, across), ("y", "z", "core", "oct")
    )
    boxes = ("y", "z", "core", "oct")
    placed = (
        P(None, boxes),
        P(boxes),
        P(None, boxes),
        P(None, boxes),
        P(boxes),
        P(boxes),
        P(),
        P(),
        P(),
        P(),
        P(),
    )
    return jax.shard_map(
        shards, mesh=torus, in_specs=placed, out_specs=P(None, boxes), check_vma=False
    )
```

```python
import jax
import jax.numpy as jnp
from jax import lax
from jax.experimental import pallas as pl
from jax.experimental.pallas import tpu as pltpu
from jax.sharding import Mesh, PartitionSpec as P

REACH = 3
COARSE = 64
LANES = 128
WIDE = 256
PAD = 8
TILE = 256
DEPTH = 2
PART = 80
FAR_MIB = 40
NEAR = ("y", "oct")
OTHER = ("z", "core")
CURVE = ("y", "z", "core")
NT = (((1,), (1,)), ((), ()))
BF16 = jnp.bfloat16
F32 = jnp.float32

VMEM = pl.BlockSpec(memory_space=pltpu.VMEM)
SMEM = pl.BlockSpec(memory_space=pltpu.SMEM)
HBM = pl.BlockSpec(memory_space=pltpu.HBM)


def params(mib):
    return pltpu.CompilerParams(vmem_limit_bytes=mib * 2**20)


def cost(flops, bytes_accessed):
    return pl.CostEstimate(flops=flops, bytes_accessed=bytes_accessed, transcendentals=0)


def passed_along(block, axis, distance):
    devices = range(lax.axis_size(axis))
    route = [(i - distance, i) for i in devices if i - distance in devices]
    return lax.ppermute(block, axis, route)


def split_rows(columns):
    points, n = columns.shape
    first = columns[:LANES].T
    rest = jnp.concatenate([columns[LANES:], jnp.zeros((WIDE - points, n), F32)], axis=0)
    return first, rest.T


def picked_rows(load, count):
    sublane = lax.broadcasted_iota(jnp.int32, (8, LANES), 0)
    past = [sublane >= 2 * k for k in range(4)]
    for group in range(count // 4):
        merged = load(4 * group, 0)
        for k in range(1, 4):
            merged = jnp.where(past[k], load(4 * group + k, k), merged)
        yield group, merged


def local_kernel(
    leaf_hbm, occ_hbm, rows_hbm, code_hbm, group_hbm, m2m_hbm, up_hbm, table_hbm, partial_ref, *rest
):
    packets = rest[: 2 * REACH]
    table_ref, table_sem, padded, chosen, leaf_ref, occ_ref, rows_ref, code_ref, group_ref, m2m_ref, up_ref, sems = rest[
        2 * REACH :
    ]
    copies = [
        pltpu.make_async_copy(source, target, sems.at[n])
        for n, (source, target) in enumerate(
            [
                (occ_hbm, occ_ref),
                (leaf_hbm, leaf_ref),
                (rows_hbm, rows_ref),
                (code_hbm, code_ref),
                (group_hbm, group_ref),
                (m2m_hbm, m2m_ref),
                (up_hbm, up_ref),
            ]
        )
    ]
    for copy in copies:
        copy.start()
    points, slots = leaf_ref.shape
    parents = code_ref.shape[1]
    ghost = rows_ref.shape[1]
    padded[pl.ds(0, PAD), :] = jnp.zeros((PAD, LANES), F32)
    padded[pl.ds(PAD + 2 * slots, PAD), :] = jnp.zeros((PAD, LANES), F32)
    copies[0].wait()
    copies[1].wait()
    for c in range(0, slots, TILE):
        scale = occ_ref[:, c : c + TILE].astype(F32) * 0.03125
        charged = (leaf_ref[:, c : c + TILE].astype(F32) * scale).astype(BF16).astype(F32)
        first, second = split_rows(charged)
        padded[pl.ds(PAD + 2 * c, TILE, stride=2), :] = first
        padded[pl.ds(PAD + 2 * c + 1, TILE, stride=2), :] = second
        table_ref[pl.ds(c, TILE), :] = first
        table_ref[pl.ds(slots + c, TILE), :] = second
    table_copy = pltpu.make_async_copy(table_ref, table_hbm, table_sem)
    table_copy.start()
    copies[2].wait()

    def one_offset(q, carry):
        base = pl.multiple_of(q * 2 * ghost, 2 * ghost)
        for group, rows in picked_rows(
            lambda n, k: padded[pl.ds(rows_ref[q, n] * 2 + (PAD - 2 * k), 8), :], ghost
        ):
            chosen[pl.ds(base + 8 * group, 8), :] = rows
        return carry

    lax.fori_loop(0, 2 * REACH, one_offset, 0)
    for q in range(2 * REACH):
        first = chosen[pl.ds(q * 2 * ghost, ghost, stride=2), :].T
        second = chosen[pl.ds(q * 2 * ghost + 1, ghost, stride=2), :].T
        packets[q][...] = jnp.concatenate([first, second[: points - LANES]], axis=0).astype(BF16)
    for copy in copies[3:]:
        copy.wait()
    parent = jnp.zeros((points, parents), F32)
    for k in range(8):
        first = table_ref[pl.ds(k, parents, stride=8), :]
        second = table_ref[pl.ds(slots + k, parents, stride=8), :]
        child = jnp.concatenate([first, second], axis=1).astype(BF16)[:, :points]
        parent += lax.dot_general(m2m_ref[k], child, NT, preferred_element_type=F32)
    parent = parent.astype(BF16).astype(F32)
    code = code_ref[...]
    lifted = jnp.zeros((points, parents), F32)
    for k in range(8):
        mine = jnp.where(code == k, parent, 0.0).astype(BF16)
        lifted += jnp.dot(up_ref[k], mine, preferred_element_type=F32)
    high = lifted.astype(BF16)
    low = (lifted - high.astype(F32)).astype(BF16)
    group = lax.broadcasted_iota(jnp.int32, (2 * COARSE, parents), 0)
    left = jnp.where(group == group_ref[...], 1.0, 0.0).astype(BF16)
    right = jnp.where(group - COARSE == group_ref[...], 1.0, 0.0).astype(BF16)

    def summed(member):
        return lax.dot_general(high, member, NT, preferred_element_type=F32) + lax.dot_general(
            low, member, NT, preferred_element_type=F32
        )

    top = PART
    below = jnp.concatenate(
        [summed(right)[top:], jnp.zeros((2 * top - points, 2 * COARSE), F32)], axis=0
    )
    partial = summed(left)[:top] + below
    for n in range(partial_ref.shape[0]):
        partial_ref[n] = partial
    table_copy.wait()


def near_kernel(parts_ref, sum_ref):
    sum_ref[...] = jnp.sum(parts_ref[...], axis=0)


def down_kernel(*refs):
    sources, out_ref, targets, (lowered_ref, sems) = refs[:8], refs[8], refs[9:17], refs[17:]
    coarse_ref, list_ref, m2l_ref, group_ref, code_ref, l2l_ref, far_ref, occ_ref = targets
    copies = [
        pltpu.make_async_copy(source, target, sems.at[n])
        for n, (source, target) in enumerate(zip(sources, targets))
    ]
    for copy in copies:
        copy.start()
    for copy in copies:
        copy.wait()
    offsets, points, _ = m2l_ref.shape
    parents = code_ref.shape[1]
    slots = out_ref.shape[1]
    coarse = jnp.sum(coarse_ref[...], axis=0).astype(BF16)
    wanted = list_ref[...]
    wanted = jnp.where(wanted == COARSE, 4 * COARSE, wanted)
    row = lax.broadcasted_iota(jnp.int32, (2 * COARSE, wanted.shape[1]), 0)
    left = jnp.where(row == wanted, 1.0, 0.0).astype(BF16)
    right = jnp.where(row - COARSE == wanted, 1.0, 0.0).astype(BF16)
    upper = jnp.dot(coarse, left, preferred_element_type=F32)
    lower = jnp.dot(coarse, right, preferred_element_type=F32)
    partners = jnp.concatenate([upper, lower[: points - PART]], axis=0).astype(BF16)
    sums = [jnp.zeros((points, 2 * COARSE), F32) for _ in range(2)]
    for r in range(offsets):
        at = (r // 2) * 2 * COARSE
        sums[r % 2] += jnp.dot(
            m2l_ref[r], partners[:, at : at + 2 * COARSE], preferred_element_type=F32
        )
    local = (sums[0][:, :COARSE] + sums[1][:, COARSE:]).astype(BF16)
    member = lax.broadcasted_iota(jnp.int32, (COARSE, parents), 0) == group_ref[...]
    pulled = jnp.dot(local, jnp.where(member, 1.0, 0.0).astype(BF16), preferred_element_type=F32)
    code = code_ref[...]
    parent = jnp.zeros((points, parents), F32)
    for k in range(8):
        mine = jnp.where(code == k, pulled, 0.0).astype(BF16)
        parent += jnp.dot(l2l_ref[k], mine, preferred_element_type=F32)
    parent = parent.astype(BF16).astype(F32)
    first, second = split_rows(parent)
    parent_rows = jnp.concatenate([first, second], axis=1).astype(BF16)[:, :points]
    for k in range(8):
        lowered = lax.dot_general(parent_rows, l2l_ref[k], NT, preferred_element_type=F32)
        lowered = jnp.concatenate([lowered, jnp.zeros((parents, WIDE - points), F32)], axis=1)
        lowered_ref[pl.ds(k, parents, stride=8), :] = lowered[:, :LANES]
        lowered_ref[pl.ds(8 * parents + k, parents, stride=8), :] = lowered[:, LANES:]

    def whole(at):
        rows = pl.ds(at, TILE)
        return (far_ref[rows, :] + lowered_ref[rows, :]).T

    for c in range(0, slots, TILE):
        both = jnp.concatenate([whole(c), whole(slots + c)[: points - LANES]], axis=0)
        live = occ_ref[:, c : c + TILE] > 0
        out_ref[:, c : c + TILE] = jnp.where(live, both, 0.0).astype(BF16)


def parity_split(rows):
    rows = rows.astype(BF16)
    even = lax.rem(lax.broadcasted_iota(jnp.int32, rows.shape, 0), 2) == 0
    zero = jnp.zeros((), BF16)
    return jnp.concatenate([jnp.where(even, rows, zero), jnp.where(even, zero, rows)], axis=1)


def gather_and_translate(accs, windows, window_sems, index, table, m2l_ref, totals):
    points = m2l_ref.shape[1]
    tiles = totals[0].shape[0] // (2 * TILE)
    steps = (m2l_ref.shape[0] // 2) * tiles // 2

    def window_copy(step, slot):
        rows = pl.ds(pl.multiple_of(step * 8, 8), 8)
        return pltpu.make_async_copy(index.at[rows], windows[slot], window_sems.at[slot])

    def load_operators(pair):
        for half in range(2):
            operator = m2l_ref[2 * pair + half].astype(F32)
            operator = jnp.concatenate([operator, jnp.zeros((WIDE - points, points), F32)], axis=0)
            operator = jnp.concatenate([operator, jnp.zeros((WIDE, WIDE - points), F32)], axis=1)
            pltpu.matmul_push_rhs(operator.astype(BF16), 0, half, transpose=True)
            blank = jnp.zeros((2 * TILE, WIDE), BF16)
            pltpu.matmul_acc_lhs(accs[0][half], blank, load_staged_rhs=0)
            totals[1][pl.ds(0, 2 * TILE), :] += pltpu.matmul_pop(accs[0][half])[:, LANES:]

    def gather(slot, which):
        window = windows[slot]

        def load(n, k):
            start = pl.multiple_of(window[4 * which + n // LANES, n % LANES], 8)
            return table[pl.ds(start, 8), :]

        merged = [rows for _, rows in picked_rows(load, 2 * TILE)]
        half = len(merged) // 2
        for n in range(2):
            rows = jnp.concatenate(merged[n * half : (n + 1) * half], axis=0)
            pltpu.matmul_acc_lhs(accs[which][n], parity_split(rows))

    def collect(tile, which):
        rows = pl.ds(pl.multiple_of(lax.rem(tile, tiles) * 2 * TILE, 2 * TILE), 2 * TILE)
        both = pltpu.matmul_pop(accs[which][0]) + pltpu.matmul_pop(accs[which][1])
        totals[0][rows, :] += both[:, :LANES]
        totals[1][rows, :] += both[:, LANES:]

    for slot in range(DEPTH):
        window_copy(slot, slot).start()
    load_operators(0)
    for half in range(2):
        pltpu.matmul_acc_lhs(accs[1][half], jnp.zeros((2 * TILE, WIDE), BF16))

    def some_steps(n, carry):
        for slot in range(DEPTH):
            step = n * DEPTH + slot
            if slot == 0:

                @pl.when((lax.rem(2 * step, tiles) == 0) & (step > 0))
                def _():
                    load_operators(2 * step // tiles)

            window_copy(step, slot).wait()
            gather(slot, 0)
            collect(jnp.maximum(2 * step - 1, 0), 1)
            gather(slot, 1)
            collect(2 * step, 0)
            window_copy(jnp.minimum(step + DEPTH, steps - 1), slot).start()
        return carry

    lax.fori_loop(0, steps // DEPTH, some_steps, 0)
    collect(2 * steps - 1, 1)
    for slot in range(DEPTH):
        window_copy(steps - 1, slot).wait()


def far_kernel(*refs):
    count = 3 + 2 * REACH
    sources, out_ref, targets = refs[:count], refs[count], refs[count + 1 : 2 * count + 1]
    table, index, total_a, total_b, *rest = refs[2 * count + 1 :]
    windows, (sems, window_sems) = rest[:DEPTH], rest[DEPTH:]
    lists, halves, *ghosts = targets[: 2 + 2 * REACH]
    (m2l_ref,) = targets[2 + 2 * REACH :]
    copies = [
        pltpu.make_async_copy(source, target, sems.at[n])
        for n, (source, target) in enumerate(zip(sources, targets))
    ]
    for copy in copies:
        copy.start()
    offsets, points, _ = m2l_ref.shape
    ghost = ghosts[0].shape[1]
    slots = out_ref.shape[0] // 2
    tiles = slots // TILE

    def spread(first_box, first, second):
        for sublane in range(8):
            at = pl.ds(first_box * 8 + sublane, TILE, stride=8)
            table[at, :] = second if sublane % 2 else first

    total_a[...] = jnp.zeros_like(total_a)
    total_b[...] = jnp.zeros_like(total_b)
    table[pl.ds(8 * (slots + 2 * REACH * ghost), 8), :] = jnp.zeros((8, LANES), F32)
    copies[0].wait()
    blocks = TILE // LANES

    def one_tile(bt, carry):
        for r in range(offsets):
            for j in range(blocks):
                column = pl.multiple_of(bt * TILE + j * LANES, LANES)
                row = (((r // 2) * tiles + bt) * 2 + r % 2) * blocks + j
                index[pl.ds(row, 1), :] = lists[r : r + 1, pl.ds(column, LANES)] * 8
        return carry

    lax.fori_loop(0, tiles, one_tile, 0)
    copies[1].wait()

    def own_tile(n, carry):
        at = pl.multiple_of(n * TILE, TILE)
        spread(at, halves[pl.ds(at, TILE), :], halves[pl.ds(slots + at, TILE), :])
        return carry

    lax.fori_loop(0, tiles, own_tile, 0)
    for q in range(2 * REACH):
        copies[2 + q].wait()
        spread(slots + q * ghost, *split_rows(ghosts[q][...].astype(F32)))
    for copy in copies[2 + 2 * REACH :]:
        copy.wait()
    pl.run_scoped(
        lambda *accs: gather_and_translate(
            (accs[:2], accs[2:]), windows, window_sems, index, table, m2l_ref, (total_a, total_b)
        ),
        *[pltpu.ACC(n % 2)((2 * TILE, WIDE), F32) for n in range(4)],
    )

    for n, total in enumerate((total_a, total_b)):
        even, odd = (total[pl.ds(part, slots, stride=2), :] for part in range(2))
        out_ref[pl.ds(n * slots, slots), :] = even + odd


def shards(
    leaf_mult,
    occupancy,
    ghost_rows,
    m2l_list,
    par_code,
    coarse_of,
    coarse_list,
    m2m,
    coarse_up,
    m2l,
    l2l,
):
    points, slots = leaf_mult.shape
    parents = slots // 8
    offsets = m2l.shape[0]
    ghost = ghost_rows.shape[1]
    shape = jax.ShapeDtypeStruct
    occ = occupancy.reshape(1, slots)
    code = par_code.reshape(1, parents)
    group_of = coarse_of.reshape(1, parents)

    near_devices = lax.axis_size(NEAR)
    table, partial, *packets = pl.pallas_call(
        local_kernel,
        out_shape=[shape((2 * slots, LANES), F32), shape((near_devices, PART, 2 * COARSE), F32)]
        + [shape((points, ghost), BF16)] * (2 * REACH),
        in_specs=[HBM] * 7,
        out_specs=[HBM] + [VMEM] * (1 + 2 * REACH),
        scratch_shapes=[
            pltpu.VMEM((2 * slots, LANES), F32),
            pltpu.SemaphoreType.DMA,
            pltpu.VMEM((2 * slots + 2 * PAD, LANES), F32),
            pltpu.VMEM((4 * REACH * ghost, LANES), F32),
            pltpu.VMEM(leaf_mult.shape, BF16),
            pltpu.VMEM(occ.shape, jnp.int32),
            pltpu.SMEM(ghost_rows.shape, jnp.int32),
            pltpu.VMEM(code.shape, jnp.int32),
            pltpu.VMEM(group_of.shape, jnp.int32),
            pltpu.VMEM(m2m.shape, BF16),
            pltpu.VMEM(coarse_up.shape, BF16),
            pltpu.SemaphoreType.DMA((7,)),
        ],
        compiler_params=params(60),
        cost_estimate=cost(10**9, 2**22),
        name="local",
    )(leaf_mult, occ, ghost_rows, code, group_of, m2m, coarse_up)
    near = lax.all_to_all(partial, NEAR, 0, 0, tiled=True)
    near = pl.pallas_call(
        near_kernel,
        out_shape=shape(near.shape[1:], F32),
        in_specs=[VMEM],
        out_specs=VMEM,
        compiler_params=params(8),
        cost_estimate=cost(10**6, 2**18),
        name="near",
    )(near)
    everywhere = lax.all_gather(near, OTHER)
    packets, near = lax.optimization_barrier((packets, near))
    stride_list = [stride for stride in range(-REACH, REACH + 1) if stride != 0]
    ghosts = [passed_along(packets[n], CURVE, stride) for n, stride in enumerate(stride_list)]
    sources = (m2l_list, table, *ghosts, m2l)
    far = pl.pallas_call(
        far_kernel,
        out_shape=shape((2 * slots, LANES), F32),
        in_specs=[HBM] * len(sources),
        out_specs=VMEM,
        scratch_shapes=[pltpu.VMEM(source.shape, source.dtype) for source in sources]
        + [
            pltpu.VMEM((8 * (slots + 2 * REACH * ghost + 1), LANES), F32),
            pltpu.VMEM((offsets * slots // LANES, LANES), jnp.int32),
            pltpu.VMEM((2 * slots, LANES), F32),
            pltpu.VMEM((2 * slots, LANES), F32),
        ]
        + [pltpu.SMEM((4 * TILE // LANES, LANES), jnp.int32)] * DEPTH
        + [
            pltpu.SemaphoreType.DMA((len(sources),)),
            pltpu.SemaphoreType.DMA((DEPTH,)),
        ],
        compiler_params=params(FAR_MIB),
        cost_estimate=cost(10**3, 2**10),
        name="far",
    )(*sources)
    wanted = coarse_list.reshape(1, -1)
    sources = (everywhere, wanted, m2l, group_of, code, l2l, far, occ)
    return pl.pallas_call(
        down_kernel,
        out_shape=shape((points, slots), BF16),
        in_specs=[HBM] * len(sources),
        out_specs=VMEM,
        scratch_shapes=[pltpu.VMEM(source.shape, source.dtype) for source in sources]
        + [pltpu.VMEM((2 * slots, LANES), F32), pltpu.SemaphoreType.DMA((len(sources),))],
        compiler_params=params(24),
        cost_estimate=cost(10**9, 2**23),
        name="down",
    )(*sources)


def solution(mesh):
    along, across = mesh.devices.shape
    rows = 4 if along % 32 == 0 else 1
    torus = Mesh(mesh.devices.reshape(rows, along // rows // 2, 2, across), CURVE + ("oct",))
    boxes = CURVE + ("oct",)
    placed = (
        P(None, boxes),
        P(boxes),
        P(None, boxes),
        P(None, boxes),
        P(boxes),
        P(boxes),
        P(),
        P(),
        P(),
        P(),
        P(),
    )
    return jax.shard_map(
        shards, mesh=torus, in_specs=placed, out_specs=P(None, boxes), check_vma=False
    )
```

```python
import jax
import jax.numpy as jnp
from jax import lax
from jax.experimental import pallas as pl
from jax.experimental.pallas import tpu as pltpu
from jax.sharding import Mesh, PartitionSpec as P

REACH = 3
COARSE = 64
LANES = 128
WIDE = 256
PAD = 8
TILE = 256
DEPTH = 2
PART = 80
FAR_MIB = 40
NEAR = ("y", "oct")
OTHER = ("z", "core")
CURVE = ("y", "z", "core")
NT = (((1,), (1,)), ((), ()))
BF16 = jnp.bfloat16
F32 = jnp.float32

VMEM = pl.BlockSpec(memory_space=pltpu.VMEM)
SMEM = pl.BlockSpec(memory_space=pltpu.SMEM)
HBM = pl.BlockSpec(memory_space=pltpu.HBM)


def params(mib):
    return pltpu.CompilerParams(vmem_limit_bytes=mib * 2**20)


def cost(flops, bytes_accessed):
    return pl.CostEstimate(flops=flops, bytes_accessed=bytes_accessed, transcendentals=0)


def passed_along(block, axis, distance):
    devices = range(lax.axis_size(axis))
    route = [(i - distance, i) for i in devices if i - distance in devices]
    return lax.ppermute(block, axis, route)


def split_rows(columns):
    points, n = columns.shape
    first = columns[:LANES].T
    rest = jnp.concatenate([columns[LANES:], jnp.zeros((WIDE - points, n), F32)], axis=0)
    return first, rest.T


def picked_rows(load, count):
    sublane = lax.broadcasted_iota(jnp.int32, (8, LANES), 0)
    past = [sublane >= 2 * k for k in range(4)]
    for group in range(count // 4):
        merged = load(4 * group, 0)
        for k in range(1, 4):
            merged = jnp.where(past[k], load(4 * group + k, k), merged)
        yield group, merged


def local_kernel(
    leaf_hbm, occ_hbm, rows_hbm, code_hbm, group_hbm, m2m_hbm, up_hbm, table_hbm, partial_ref, *rest
):
    packets = rest[: 2 * REACH]
    table_ref, table_sem, padded, chosen, leaf_ref, occ_ref, rows_ref, code_ref, group_ref, m2m_ref, up_ref, sems = rest[
        2 * REACH :
    ]
    copies = [
        pltpu.make_async_copy(source, target, sems.at[n])
        for n, (source, target) in enumerate(
            [
                (occ_hbm, occ_ref),
                (leaf_hbm, leaf_ref),
                (rows_hbm, rows_ref),
                (code_hbm, code_ref),
                (group_hbm, group_ref),
                (m2m_hbm, m2m_ref),
                (up_hbm, up_ref),
            ]
        )
    ]
    for copy in copies:
        copy.start()
    points, slots = leaf_ref.shape
    parents = code_ref.shape[1]
    ghost = rows_ref.shape[1]
    padded[pl.ds(0, PAD), :] = jnp.zeros((PAD, LANES), F32)
    padded[pl.ds(PAD + 2 * slots, PAD), :] = jnp.zeros((PAD, LANES), F32)
    copies[0].wait()
    copies[1].wait()
    for c in range(0, slots, TILE):
        scale = occ_ref[:, c : c + TILE].astype(F32) * 0.03125
        charged = (leaf_ref[:, c : c + TILE].astype(F32) * scale).astype(BF16).astype(F32)
        first, second = split_rows(charged)
        padded[pl.ds(PAD + 2 * c, TILE, stride=2), :] = first
        padded[pl.ds(PAD + 2 * c + 1, TILE, stride=2), :] = second
        table_ref[pl.ds(c, TILE), :] = first
        table_ref[pl.ds(slots + c, TILE), :] = second
    table_copy = pltpu.make_async_copy(table_ref, table_hbm, table_sem)
    table_copy.start()
    copies[2].wait()

    def one_offset(q, carry):
        base = pl.multiple_of(q * 2 * ghost, 2 * ghost)
        for group, rows in picked_rows(
            lambda n, k: padded[pl.ds(rows_ref[q, n] * 2 + (PAD - 2 * k), 8), :], ghost
        ):
            chosen[pl.ds(base + 8 * group, 8), :] = rows
        return carry

    lax.fori_loop(0, 2 * REACH, one_offset, 0)
    for q in range(2 * REACH):
        first = chosen[pl.ds(q * 2 * ghost, ghost, stride=2), :].T
        second = chosen[pl.ds(q * 2 * ghost + 1, ghost, stride=2), :].T
        packets[q][...] = jnp.concatenate([first, second[: points - LANES]], axis=0).astype(BF16)
    for copy in copies[3:]:
        copy.wait()
    parent = jnp.zeros((points, parents), F32)
    for k in range(8):
        first = table_ref[pl.ds(k, parents, stride=8), :]
        second = table_ref[pl.ds(slots + k, parents, stride=8), :]
        child = jnp.concatenate([first, second], axis=1).astype(BF16)[:, :points]
        parent += lax.dot_general(m2m_ref[k], child, NT, preferred_element_type=F32)
    parent = parent.astype(BF16).astype(F32)
    code = code_ref[...]
    lifted = jnp.zeros((points, parents), F32)
    for k in range(8):
        mine = jnp.where(code == k, parent, 0.0).astype(BF16)
        lifted += jnp.dot(up_ref[k], mine, preferred_element_type=F32)
    high = lifted.astype(BF16)
    low = (lifted - high.astype(F32)).astype(BF16)
    group = lax.broadcasted_iota(jnp.int32, (2 * COARSE, parents), 0)
    left = jnp.where(group == group_ref[...], 1.0, 0.0).astype(BF16)
    right = jnp.where(group - COARSE == group_ref[...], 1.0, 0.0).astype(BF16)

    def summed(member):
        return lax.dot_general(high, member, NT, preferred_element_type=F32) + lax.dot_general(
            low, member, NT, preferred_element_type=F32
        )

    top = PART
    below = jnp.concatenate(
        [summed(right)[top:], jnp.zeros((2 * top - points, 2 * COARSE), F32)], axis=0
    )
    partial_ref[pl.ds(0, top), :] = summed(left)[:top] + below
    partial_ref[pl.ds(top, LANES - top), :] = jnp.zeros((LANES - top, LANES), F32)
    table_copy.wait()


def near_kernel(parts_ref, sum_ref):
    total = jnp.sum(parts_ref[...], axis=0)
    for n in range(sum_ref.shape[0]):
        sum_ref[n] = total


def summed_parts(parts, copies, name):
    return pl.pallas_call(
        near_kernel,
        out_shape=jax.ShapeDtypeStruct((copies,) + parts.shape[1:], F32),
        in_specs=[VMEM],
        out_specs=VMEM,
        compiler_params=params(8),
        cost_estimate=cost(10**6, 2**18),
        name=name,
    )(parts)


def down_kernel(*refs):
    sources, lowered_ref, targets, sems = refs[:6], refs[6], refs[7:13], refs[13]
    coarse_ref, list_ref, m2l_ref, group_ref, code_ref, l2l_ref = targets
    copies = [
        pltpu.make_async_copy(source, target, sems.at[n])
        for n, (source, target) in enumerate(zip(sources, targets))
    ]
    for copy in copies:
        copy.start()
    for copy in copies:
        copy.wait()
    offsets, points, _ = m2l_ref.shape
    parents = code_ref.shape[1]
    coarse = coarse_ref[...].reshape(-1, 2 * COARSE)[:PART].astype(BF16)
    wanted = list_ref[...]
    wanted = jnp.where(wanted == COARSE, 4 * COARSE, wanted)
    row = lax.broadcasted_iota(jnp.int32, (2 * COARSE, wanted.shape[1]), 0)
    left = jnp.where(row == wanted, 1.0, 0.0).astype(BF16)
    right = jnp.where(row - COARSE == wanted, 1.0, 0.0).astype(BF16)
    upper = jnp.dot(coarse, left, preferred_element_type=F32)
    lower = jnp.dot(coarse, right, preferred_element_type=F32)
    partners = jnp.concatenate([upper, lower[: points - PART]], axis=0).astype(BF16)
    sums = [jnp.zeros((points, 2 * COARSE), F32) for _ in range(2)]
    for r in range(offsets):
        at = (r // 2) * 2 * COARSE
        sums[r % 2] += jnp.dot(
            m2l_ref[r], partners[:, at : at + 2 * COARSE], preferred_element_type=F32
        )
    local = (sums[0][:, :COARSE] + sums[1][:, COARSE:]).astype(BF16)
    member = lax.broadcasted_iota(jnp.int32, (COARSE, parents), 0) == group_ref[...]
    pulled = jnp.dot(local, jnp.where(member, 1.0, 0.0).astype(BF16), preferred_element_type=F32)
    code = code_ref[...]
    parent = jnp.zeros((points, parents), F32)
    for k in range(8):
        mine = jnp.where(code == k, pulled, 0.0).astype(BF16)
        parent += jnp.dot(l2l_ref[k], mine, preferred_element_type=F32)
    parent = parent.astype(BF16).astype(F32)
    first, second = split_rows(parent)
    parent_rows = jnp.concatenate([first, second], axis=1).astype(BF16)[:, :points]
    for k in range(8):
        lowered = lax.dot_general(parent_rows, l2l_ref[k], NT, preferred_element_type=F32)
        lowered = jnp.concatenate([lowered, jnp.zeros((parents, WIDE - points), F32)], axis=1)
        lowered_ref[pl.ds(k, parents, stride=8), :] = lowered[:, :LANES]
        lowered_ref[pl.ds(8 * parents + k, parents, stride=8), :] = lowered[:, LANES:]


def parity_split(rows):
    rows = rows.astype(BF16)
    even = lax.rem(lax.broadcasted_iota(jnp.int32, rows.shape, 0), 2) == 0
    zero = jnp.zeros((), BF16)
    return jnp.concatenate([jnp.where(even, rows, zero), jnp.where(even, zero, rows)], axis=1)


def gather_and_translate(accs, windows, window_sems, index, table, m2l_ref, totals):
    points = m2l_ref.shape[1]
    tiles = totals[0].shape[0] // (2 * TILE)
    steps = (m2l_ref.shape[0] // 2) * tiles // 2

    def window_copy(step, slot):
        rows = pl.ds(pl.multiple_of(step * 8, 8), 8)
        return pltpu.make_async_copy(index.at[rows], windows[slot], window_sems.at[slot])

    def load_operators(pair):
        for half in range(2):
            operator = m2l_ref[2 * pair + half].astype(F32)
            operator = jnp.concatenate([operator, jnp.zeros((WIDE - points, points), F32)], axis=0)
            operator = jnp.concatenate([operator, jnp.zeros((WIDE, WIDE - points), F32)], axis=1)
            pltpu.matmul_push_rhs(operator.astype(BF16), 0, half, transpose=True)
            blank = jnp.zeros((2 * TILE, WIDE), BF16)
            pltpu.matmul_acc_lhs(accs[0][half], blank, load_staged_rhs=0)
            totals[1][pl.ds(0, 2 * TILE), :] += pltpu.matmul_pop(accs[0][half])[:, LANES:]

    def gather(slot, which):
        window = windows[slot]

        def load(n, k):
            start = pl.multiple_of(window[4 * which + n // LANES, n % LANES], 8)
            return pltpu.annotate(table, no_bank_conflict=True)[pl.ds(start, 8), :]

        merged = [rows for _, rows in picked_rows(load, 2 * TILE)]
        half = len(merged) // 2
        for n in range(2):
            rows = jnp.concatenate(merged[n * half : (n + 1) * half], axis=0)
            pltpu.matmul_acc_lhs(accs[which][n], parity_split(rows))

    def collect(tile, which):
        rows = pl.ds(pl.multiple_of(lax.rem(tile, tiles) * 2 * TILE, 2 * TILE), 2 * TILE)
        both = pltpu.matmul_pop(accs[which][0]) + pltpu.matmul_pop(accs[which][1])
        totals[0][rows, :] += both[:, :LANES]
        totals[1][rows, :] += both[:, LANES:]

    for slot in range(DEPTH):
        window_copy(slot, slot).start()
    load_operators(0)
    for half in range(2):
        pltpu.matmul_acc_lhs(accs[1][half], jnp.zeros((2 * TILE, WIDE), BF16))

    def some_steps(n, carry):
        for slot in range(DEPTH):
            step = n * DEPTH + slot
            if slot == 0:

                @pl.when((lax.rem(2 * step, tiles) == 0) & (step > 0))
                def _():
                    load_operators(2 * step // tiles)

            window_copy(step, slot).wait()
            gather(slot, 0)
            collect(jnp.maximum(2 * step - 1, 0), 1)
            gather(slot, 1)
            collect(2 * step, 0)
            window_copy(jnp.minimum(step + DEPTH, steps - 1), slot).start()
        return carry

    lax.fori_loop(0, steps // DEPTH, some_steps, 0)
    collect(2 * steps - 1, 1)
    for slot in range(DEPTH):
        window_copy(steps - 1, slot).wait()


def far_kernel(*refs):
    count = 5 + 2 * REACH
    sources, out_ref, targets = refs[:count], refs[count], refs[count + 1 : 2 * count + 1]
    table, index, total_a, total_b, *rest = refs[2 * count + 1 :]
    windows, (sems, window_sems) = rest[:DEPTH], rest[DEPTH:]
    lists, halves, *ghosts = targets[: 2 + 2 * REACH]
    m2l_ref, occ_ref, lowered_ref = targets[2 + 2 * REACH :]
    copies = [
        pltpu.make_async_copy(source, target, sems.at[n])
        for n, (source, target) in enumerate(zip(sources, targets))
    ]
    for copy in copies:
        copy.start()
    offsets, points, _ = m2l_ref.shape
    ghost = ghosts[0].shape[1]
    slots = out_ref.shape[1]
    tiles = slots // TILE

    def spread(first_box, first, second):
        for sublane in range(8):
            at = pl.ds(first_box * 8 + sublane, TILE, stride=8)
            table[at, :] = second if sublane % 2 else first

    total_a[...] = jnp.zeros_like(total_a)
    total_b[...] = jnp.zeros_like(total_b)
    table[pl.ds(8 * (slots + 2 * REACH * ghost), 8), :] = jnp.zeros((8, LANES), F32)
    copies[0].wait()
    blocks = TILE // LANES

    def one_tile(bt, carry):
        for r in range(offsets):
            for j in range(blocks):
                column = pl.multiple_of(bt * TILE + j * LANES, LANES)
                row = (((r // 2) * tiles + bt) * 2 + r % 2) * blocks + j
                index[pl.ds(row, 1), :] = lists[r : r + 1, pl.ds(column, LANES)] * 8
        return carry

    lax.fori_loop(0, tiles, one_tile, 0)
    copies[1].wait()

    def own_tile(n, carry):
        at = pl.multiple_of(n * TILE, TILE)
        spread(at, halves[pl.ds(at, TILE), :], halves[pl.ds(slots + at, TILE), :])
        return carry

    lax.fori_loop(0, tiles, own_tile, 0)
    for q in range(2 * REACH):
        copies[2 + q].wait()
        spread(slots + q * ghost, *split_rows(ghosts[q][...].astype(F32)))
    for copy in copies[2 + 2 * REACH :]:
        copy.wait()
    pl.run_scoped(
        lambda *accs: gather_and_translate(
            (accs[:2], accs[2:]), windows, window_sems, index, table, m2l_ref, (total_a, total_b)
        ),
        *[pltpu.ACC(n % 2)((2 * TILE, WIDE), F32) for n in range(4)],
    )

    def whole(total, at, c):
        even, odd = (total[pl.ds(2 * c + part, TILE, stride=2), :] for part in range(2))
        return (even + odd + lowered_ref[pl.ds(at + c, TILE), :]).T

    for c in range(0, slots, TILE):
        second = whole(total_b, slots, c)[: points - LANES]
        both = jnp.concatenate([whole(total_a, 0, c), second], axis=0)
        live = occ_ref[:, c : c + TILE] > 0
        out_ref[:, c : c + TILE] = jnp.where(live, both, 0.0).astype(BF16)


def shards(
    leaf_mult,
    occupancy,
    ghost_rows,
    m2l_list,
    par_code,
    coarse_of,
    coarse_list,
    m2m,
    coarse_up,
    m2l,
    l2l,
):
    points, slots = leaf_mult.shape
    parents = slots // 8
    offsets = m2l.shape[0]
    ghost = ghost_rows.shape[1]
    shape = jax.ShapeDtypeStruct
    occ = occupancy.reshape(1, slots)
    code = par_code.reshape(1, parents)
    group_of = coarse_of.reshape(1, parents)

    near_devices = lax.axis_size(NEAR)
    table, partial, *packets = pl.pallas_call(
        local_kernel,
        out_shape=[shape((2 * slots, LANES), F32), shape((LANES, 2 * COARSE), F32)]
        + [shape((points, ghost), BF16)] * (2 * REACH),
        in_specs=[HBM] * 7,
        out_specs=[HBM] + [VMEM] * (1 + 2 * REACH),
        scratch_shapes=[
            pltpu.VMEM((2 * slots, LANES), F32),
            pltpu.SemaphoreType.DMA,
            pltpu.VMEM((2 * slots + 2 * PAD, LANES), F32),
            pltpu.VMEM((4 * REACH * ghost, LANES), F32),
            pltpu.VMEM(leaf_mult.shape, BF16),
            pltpu.VMEM(occ.shape, jnp.int32),
            pltpu.SMEM(ghost_rows.shape, jnp.int32),
            pltpu.VMEM(code.shape, jnp.int32),
            pltpu.VMEM(group_of.shape, jnp.int32),
            pltpu.VMEM(m2m.shape, BF16),
            pltpu.VMEM(coarse_up.shape, BF16),
            pltpu.SemaphoreType.DMA((7,)),
        ],
        compiler_params=params(60),
        cost_estimate=cost(10**9, 2**22),
        name="local",
    )(leaf_mult, occ, ghost_rows, code, group_of, m2m, coarse_up)
    slices = partial.reshape(near_devices, LANES // near_devices, 2 * COARSE)
    for group, following in ((NEAR, OTHER), (OTHER, NEAR)):
        slices = lax.all_to_all(slices, group, 0, 0, tiled=True)
        slices = summed_parts(slices, lax.axis_size(following), "sum_over_" + group[0])
    stride_list = [stride for stride in range(-REACH, REACH + 1) if stride != 0]
    ghosts = [passed_along(packets[n], CURVE, stride) for n, stride in enumerate(stride_list)]
    everywhere = lax.all_to_all(slices, NEAR, 0, 0, tiled=True)
    wanted = coarse_list.reshape(1, -1)
    sources = (everywhere, wanted, m2l, group_of, code, l2l)
    lowered = pl.pallas_call(
        down_kernel,
        out_shape=shape((2 * slots, LANES), F32),
        in_specs=[HBM] * len(sources),
        out_specs=VMEM,
        scratch_shapes=[pltpu.VMEM(source.shape, source.dtype) for source in sources]
        + [pltpu.SemaphoreType.DMA((len(sources),))],
        compiler_params=params(24),
        cost_estimate=cost(10**9, 2**23),
        name="down",
    )(*sources)
    sources = (m2l_list, table, *ghosts, m2l, occ, lowered)
    return pl.pallas_call(
        far_kernel,
        out_shape=shape((points, slots), BF16),
        in_specs=[HBM] * len(sources),
        out_specs=VMEM,
        scratch_shapes=[pltpu.VMEM(source.shape, source.dtype) for source in sources]
        + [
            pltpu.VMEM((8 * (slots + 2 * REACH * ghost + 1), LANES), F32),
            pltpu.VMEM((offsets * slots // LANES, LANES), jnp.int32),
            pltpu.VMEM((2 * slots, LANES), F32),
            pltpu.VMEM((2 * slots, LANES), F32),
        ]
        + [pltpu.SMEM((4 * TILE // LANES, LANES), jnp.int32)] * DEPTH
        + [
            pltpu.SemaphoreType.DMA((len(sources),)),
            pltpu.SemaphoreType.DMA((DEPTH,)),
        ],
        compiler_params=params(FAR_MIB),
        cost_estimate=cost(4 * 10**10, 2**24),
        name="far",
    )(*sources)


def solution(mesh):
    along, across = mesh.devices.shape
    rows = 4 if along % 32 == 0 else 1
    torus = Mesh(mesh.devices.reshape(rows, along // rows // 2, 2, across), CURVE + ("oct",))
    boxes = CURVE + ("oct",)
    placed = (
        P(None, boxes),
        P(boxes),
        P(None, boxes),
        P(None, boxes),
        P(boxes),
        P(boxes),
        P(),
        P(),
        P(),
        P(),
        P(),
    )
    return jax.shard_map(
        shards, mesh=torus, in_specs=placed, out_specs=P(None, boxes), check_vma=False
    )
```

```python
import jax
import jax.numpy as jnp
from jax import lax
from jax.experimental import pallas as pl
from jax.experimental.pallas import tpu as pltpu
from jax.sharding import Mesh, PartitionSpec as P

REACH = 3
COARSE = 64
LANES = 128
WIDE = 256
PAD = 8
TILE = 256
DEPTH = 2
PART = 80
FAR_MIB = 40
NEAR = ("y", "oct")
OTHER = ("z", "core")
CURVE = ("y", "z", "core")
NT = (((1,), (1,)), ((), ()))
BF16 = jnp.bfloat16
F32 = jnp.float32

VMEM = pl.BlockSpec(memory_space=pltpu.VMEM)
SMEM = pl.BlockSpec(memory_space=pltpu.SMEM)
HBM = pl.BlockSpec(memory_space=pltpu.HBM)


def params(mib):
    return pltpu.CompilerParams(vmem_limit_bytes=mib * 2**20)


def cost(flops, bytes_accessed):
    return pl.CostEstimate(flops=flops, bytes_accessed=bytes_accessed, transcendentals=0)


def passed_along(block, axis, distance):
    devices = range(lax.axis_size(axis))
    route = [(i - distance, i) for i in devices if i - distance in devices]
    return lax.ppermute(block, axis, route)


def split_rows(columns):
    points, n = columns.shape
    first = columns[:LANES].T
    rest = jnp.concatenate([columns[LANES:], jnp.zeros((WIDE - points, n), F32)], axis=0)
    return first, rest.T


def picked_rows(load, count):
    sublane = lax.broadcasted_iota(jnp.int32, (8, LANES), 0)
    past = [sublane >= 2 * k for k in range(4)]
    for group in range(count // 4):
        merged = load(4 * group, 0)
        for k in range(1, 4):
            merged = jnp.where(past[k], load(4 * group + k, k), merged)
        yield group, merged


def local_kernel(
    leaf_hbm, occ_hbm, rows_hbm, code_hbm, group_hbm, m2m_hbm, up_hbm, table_hbm, partial_ref, *rest
):
    packets = rest[: 2 * REACH]
    table_ref, table_sem, padded, chosen, leaf_ref, occ_ref, rows_ref, code_ref, group_ref, m2m_ref, up_ref, sems = rest[
        2 * REACH :
    ]
    copies = [
        pltpu.make_async_copy(source, target, sems.at[n])
        for n, (source, target) in enumerate(
            [
                (occ_hbm, occ_ref),
                (leaf_hbm, leaf_ref),
                (rows_hbm, rows_ref),
                (code_hbm, code_ref),
                (group_hbm, group_ref),
                (m2m_hbm, m2m_ref),
                (up_hbm, up_ref),
            ]
        )
    ]
    for copy in copies:
        copy.start()
    points, slots = leaf_ref.shape
    parents = code_ref.shape[1]
    ghost = rows_ref.shape[1]
    padded[pl.ds(0, PAD), :] = jnp.zeros((PAD, LANES), F32)
    padded[pl.ds(PAD + 2 * slots, PAD), :] = jnp.zeros((PAD, LANES), F32)
    copies[0].wait()
    copies[1].wait()
    for c in range(0, slots, TILE):
        scale = occ_ref[:, c : c + TILE].astype(F32) * 0.03125
        charged = (leaf_ref[:, c : c + TILE].astype(F32) * scale).astype(BF16).astype(F32)
        first, second = split_rows(charged)
        padded[pl.ds(PAD + 2 * c, TILE, stride=2), :] = first
        padded[pl.ds(PAD + 2 * c + 1, TILE, stride=2), :] = second
        table_ref[pl.ds(c, TILE), :] = first
        table_ref[pl.ds(slots + c, TILE), :] = second
    table_copy = pltpu.make_async_copy(table_ref, table_hbm, table_sem)
    table_copy.start()
    copies[2].wait()

    def one_offset(q, carry):
        base = pl.multiple_of(q * 2 * ghost, 2 * ghost)
        for group, rows in picked_rows(
            lambda n, k: padded[pl.ds(rows_ref[q, n] * 2 + (PAD - 2 * k), 8), :], ghost
        ):
            chosen[pl.ds(base + 8 * group, 8), :] = rows
        return carry

    lax.fori_loop(0, 2 * REACH, one_offset, 0)
    for q in range(2 * REACH):
        first = chosen[pl.ds(q * 2 * ghost, ghost, stride=2), :].T
        second = chosen[pl.ds(q * 2 * ghost + 1, ghost, stride=2), :].T
        packets[q][...] = jnp.concatenate([first, second[: points - LANES]], axis=0).astype(BF16)
    for copy in copies[3:]:
        copy.wait()
    parent = jnp.zeros((points, parents), F32)
    for k in range(8):
        first = table_ref[pl.ds(k, parents, stride=8), :]
        second = table_ref[pl.ds(slots + k, parents, stride=8), :]
        child = jnp.concatenate([first, second], axis=1).astype(BF16)[:, :points]
        parent += lax.dot_general(m2m_ref[k], child, NT, preferred_element_type=F32)
    parent = parent.astype(BF16).astype(F32)
    code = code_ref[...]
    lifted = jnp.zeros((points, parents), F32)
    for k in range(8):
        mine = jnp.where(code == k, parent, 0.0).astype(BF16)
        lifted += jnp.dot(up_ref[k], mine, preferred_element_type=F32)
    high = lifted.astype(BF16)
    low = (lifted - high.astype(F32)).astype(BF16)
    group = lax.broadcasted_iota(jnp.int32, (2 * COARSE, parents), 0)
    left = jnp.where(group == group_ref[...], 1.0, 0.0).astype(BF16)
    right = jnp.where(group - COARSE == group_ref[...], 1.0, 0.0).astype(BF16)

    def summed(member):
        return lax.dot_general(high, member, NT, preferred_element_type=F32) + lax.dot_general(
            low, member, NT, preferred_element_type=F32
        )

    top = PART
    below = jnp.concatenate(
        [summed(right)[top:], jnp.zeros((2 * top - points, 2 * COARSE), F32)], axis=0
    )
    partial_ref[pl.ds(0, top), :] = summed(left)[:top] + below
    partial_ref[pl.ds(top, LANES - top), :] = jnp.zeros((LANES - top, LANES), F32)
    table_copy.wait()


def near_kernel(parts_ref, sum_ref):
    total = jnp.sum(parts_ref[...], axis=0)
    for n in range(sum_ref.shape[0]):
        sum_ref[n] = total


def summed_parts(parts, copies, name):
    return pl.pallas_call(
        near_kernel,
        out_shape=jax.ShapeDtypeStruct((copies,) + parts.shape[1:], F32),
        in_specs=[VMEM],
        out_specs=VMEM,
        compiler_params=params(8),
        cost_estimate=cost(10**6, 2**18),
        name=name,
    )(parts)


def down_kernel(*refs):
    sources, lowered_ref, targets, sems = refs[:6], refs[6], refs[7:13], refs[13]
    coarse_ref, list_ref, m2l_ref, group_ref, code_ref, l2l_ref = targets
    copies = [
        pltpu.make_async_copy(source, target, sems.at[n])
        for n, (source, target) in enumerate(zip(sources, targets))
    ]
    for copy in copies:
        copy.start()
    for copy in copies:
        copy.wait()
    offsets, points, _ = m2l_ref.shape
    parents = code_ref.shape[1]
    coarse = coarse_ref[...].reshape(-1, 2 * COARSE)[:PART].astype(BF16)
    wanted = list_ref[...]
    wanted = jnp.where(wanted == COARSE, 4 * COARSE, wanted)
    row = lax.broadcasted_iota(jnp.int32, (2 * COARSE, wanted.shape[1]), 0)
    left = jnp.where(row == wanted, 1.0, 0.0).astype(BF16)
    right = jnp.where(row - COARSE == wanted, 1.0, 0.0).astype(BF16)
    upper = jnp.dot(coarse, left, preferred_element_type=F32)
    lower = jnp.dot(coarse, right, preferred_element_type=F32)
    partners = jnp.concatenate([upper, lower[: points - PART]], axis=0).astype(BF16)
    sums = [jnp.zeros((points, 2 * COARSE), F32) for _ in range(2)]
    for r in range(offsets):
        at = (r // 2) * 2 * COARSE
        sums[r % 2] += jnp.dot(
            m2l_ref[r], partners[:, at : at + 2 * COARSE], preferred_element_type=F32
        )
    local = (sums[0][:, :COARSE] + sums[1][:, COARSE:]).astype(BF16)
    member = lax.broadcasted_iota(jnp.int32, (COARSE, parents), 0) == group_ref[...]
    pulled = jnp.dot(local, jnp.where(member, 1.0, 0.0).astype(BF16), preferred_element_type=F32)
    code = code_ref[...]
    parent = jnp.zeros((points, parents), F32)
    for k in range(8):
        mine = jnp.where(code == k, pulled, 0.0).astype(BF16)
        parent += jnp.dot(l2l_ref[k], mine, preferred_element_type=F32)
    parent = parent.astype(BF16).astype(F32)
    first, second = split_rows(parent)
    parent_rows = jnp.concatenate([first, second], axis=1).astype(BF16)[:, :points]
    for k in range(8):
        lowered = lax.dot_general(parent_rows, l2l_ref[k], NT, preferred_element_type=F32)
        lowered = jnp.concatenate([lowered, jnp.zeros((parents, WIDE - points), F32)], axis=1)
        lowered_ref[pl.ds(k, parents, stride=8), :] = lowered[:, :LANES]
        lowered_ref[pl.ds(8 * parents + k, parents, stride=8), :] = lowered[:, LANES:]


def parity_split(rows):
    rows = rows.astype(BF16)
    even = lax.rem(lax.broadcasted_iota(jnp.int32, rows.shape, 0), 2) == 0
    zero = jnp.zeros((), BF16)
    return jnp.concatenate([jnp.where(even, rows, zero), jnp.where(even, zero, rows)], axis=1)


def gather_and_translate(accs, windows, window_sems, index, table, m2l_ref, totals):
    points = m2l_ref.shape[1]
    tiles = totals[0].shape[0] // (2 * TILE)
    steps = (m2l_ref.shape[0] // 2) * tiles // 2

    def window_copy(step, slot):
        rows = pl.ds(pl.multiple_of(step * 8, 8), 8)
        return pltpu.make_async_copy(index.at[rows], windows[slot], window_sems.at[slot])

    def load_operators(pair):
        for half in range(2):
            operator = m2l_ref[2 * pair + half].astype(F32)
            operator = jnp.concatenate([operator, jnp.zeros((WIDE - points, points), F32)], axis=0)
            operator = jnp.concatenate([operator, jnp.zeros((WIDE, WIDE - points), F32)], axis=1)
            pltpu.matmul_push_rhs(operator.astype(BF16), 0, half, transpose=True)
            blank = jnp.zeros((2 * TILE, WIDE), BF16)
            pltpu.matmul_acc_lhs(accs[0][half], blank, load_staged_rhs=0)
            totals[1][pl.ds(0, 2 * TILE), :] += pltpu.matmul_pop(accs[0][half])[:, LANES:]

    def gather(slot, which):
        window = windows[slot]

        def load(n, k):
            start = pl.multiple_of(window[4 * which + n // LANES, n % LANES], 8)
            return pltpu.annotate(table, no_bank_conflict=True)[pl.ds(start, 8), :]

        merged = [rows for _, rows in picked_rows(load, 2 * TILE)]
        half = len(merged) // 2
        for n in range(2):
            rows = jnp.concatenate(merged[n * half : (n + 1) * half], axis=0)
            pltpu.matmul_acc_lhs(accs[which][n], parity_split(rows))

    def collect(tile, which):
        rows = pl.ds(pl.multiple_of(lax.rem(tile, tiles) * 2 * TILE, 2 * TILE), 2 * TILE)
        both = pltpu.matmul_pop(accs[which][0]) + pltpu.matmul_pop(accs[which][1])
        totals[0][rows, :] += both[:, :LANES]
        totals[1][rows, :] += both[:, LANES:]

    for slot in range(DEPTH):
        window_copy(slot, slot).start()
    load_operators(0)
    for half in range(2):
        pltpu.matmul_acc_lhs(accs[1][half], jnp.zeros((2 * TILE, WIDE), BF16))

    def some_steps(n, carry):
        for slot in range(DEPTH):
            step = n * DEPTH + slot
            if slot == 0:

                @pl.when((lax.rem(2 * step, tiles) == 0) & (step > 0))
                def _():
                    load_operators(2 * step // tiles)

            window_copy(step, slot).wait()
            gather(slot, 0)
            collect(jnp.maximum(2 * step - 1, 0), 1)
            gather(slot, 1)
            collect(2 * step, 0)
            window_copy(jnp.minimum(step + DEPTH, steps - 1), slot).start()
        return carry

    lax.fori_loop(0, steps // DEPTH, some_steps, 0)
    collect(2 * steps - 1, 1)
    for slot in range(DEPTH):
        window_copy(steps - 1, slot).wait()


def far_kernel(*refs):
    count = 5 + 2 * REACH
    sources, out_ref, targets = refs[:count], refs[count], refs[count + 1 : 2 * count + 1]
    table, index, total_a, total_b, *rest = refs[2 * count + 1 :]
    windows, (sems, window_sems) = rest[:DEPTH], rest[DEPTH:]
    lists, halves, *ghosts = targets[: 2 + 2 * REACH]
    m2l_ref, occ_ref, lowered_ref = targets[2 + 2 * REACH :]
    copies = [
        pltpu.make_async_copy(source, target, sems.at[n])
        for n, (source, target) in enumerate(zip(sources, targets))
    ]
    for copy in copies:
        copy.start()
    offsets, points, _ = m2l_ref.shape
    ghost = ghosts[0].shape[1]
    slots = out_ref.shape[1]
    tiles = slots // TILE

    def spread(first_box, first, second):
        for sublane in range(8):
            at = pl.ds(first_box * 8 + sublane, TILE, stride=8)
            table[at, :] = second if sublane % 2 else first

    total_a[...] = jnp.zeros_like(total_a)
    total_b[...] = jnp.zeros_like(total_b)
    table[pl.ds(8 * (slots + 2 * REACH * ghost), 8), :] = jnp.zeros((8, LANES), F32)
    copies[0].wait()
    blocks = TILE // LANES

    def one_tile(bt, carry):
        for r in range(offsets):
            for j in range(blocks):
                column = pl.multiple_of(bt * TILE + j * LANES, LANES)
                row = (((r // 2) * tiles + bt) * 2 + r % 2) * blocks + j
                index[pl.ds(row, 1), :] = lists[r : r + 1, pl.ds(column, LANES)] * 8
        return carry

    lax.fori_loop(0, tiles, one_tile, 0)
    copies[1].wait()

    def own_tile(n, carry):
        at = pl.multiple_of(n * TILE, TILE)
        spread(at, halves[pl.ds(at, TILE), :], halves[pl.ds(slots + at, TILE), :])
        return carry

    lax.fori_loop(0, tiles, own_tile, 0)
    for q in range(2 * REACH):
        copies[2 + q].wait()
        spread(slots + q * ghost, *split_rows(ghosts[q][...].astype(F32)))
    for copy in copies[2 + 2 * REACH :]:
        copy.wait()
    pl.run_scoped(
        lambda *accs: gather_and_translate(
            (accs[:2], accs[2:]), windows, window_sems, index, table, m2l_ref, (total_a, total_b)
        ),
        *[pltpu.ACC(n % 2)((2 * TILE, WIDE), F32) for n in range(4)],
    )

    def whole(total, at, c):
        even, odd = (total[pl.ds(2 * c + part, TILE, stride=2), :] for part in range(2))
        return (even + odd + lowered_ref[pl.ds(at + c, TILE), :]).T

    for c in range(0, slots, TILE):
        second = whole(total_b, slots, c)[: points - LANES]
        both = jnp.concatenate([whole(total_a, 0, c), second], axis=0)
        live = occ_ref[:, c : c + TILE] > 0
        out_ref[:, c : c + TILE] = jnp.where(live, both, 0.0).astype(BF16)


def shards(
    leaf_mult,
    occupancy,
    ghost_rows,
    m2l_list,
    par_code,
    coarse_of,
    coarse_list,
    m2m,
    coarse_up,
    m2l,
    l2l,
):
    points, slots = leaf_mult.shape
    parents = slots // 8
    offsets = m2l.shape[0]
    ghost = ghost_rows.shape[1]
    shape = jax.ShapeDtypeStruct
    occ = occupancy.reshape(1, slots)
    code = par_code.reshape(1, parents)
    group_of = coarse_of.reshape(1, parents)

    near_devices = lax.axis_size(NEAR)
    table, partial, *packets = pl.pallas_call(
        local_kernel,
        out_shape=[shape((2 * slots, LANES), F32), shape((LANES, 2 * COARSE), F32)]
        + [shape((points, ghost), BF16)] * (2 * REACH),
        in_specs=[HBM] * 7,
        out_specs=[HBM] + [VMEM] * (1 + 2 * REACH),
        scratch_shapes=[
            pltpu.VMEM((2 * slots, LANES), F32),
            pltpu.SemaphoreType.DMA,
            pltpu.VMEM((2 * slots + 2 * PAD, LANES), F32),
            pltpu.VMEM((4 * REACH * ghost, LANES), F32),
            pltpu.VMEM(leaf_mult.shape, BF16),
            pltpu.VMEM(occ.shape, jnp.int32),
            pltpu.SMEM(ghost_rows.shape, jnp.int32),
            pltpu.VMEM(code.shape, jnp.int32),
            pltpu.VMEM(group_of.shape, jnp.int32),
            pltpu.VMEM(m2m.shape, BF16),
            pltpu.VMEM(coarse_up.shape, BF16),
            pltpu.SemaphoreType.DMA((7,)),
        ],
        compiler_params=params(60),
        cost_estimate=cost(10**9, 2**22),
        name="local",
    )(leaf_mult, occ, ghost_rows, code, group_of, m2m, coarse_up)
    slices = partial.reshape(near_devices, LANES // near_devices, 2 * COARSE)
    slices = lax.all_to_all(slices, NEAR, 0, 0, tiled=True)
    slices = summed_parts(slices, lax.axis_size(OTHER), "sum_over_y")
    packets, slices = lax.optimization_barrier((packets, slices))
    slices = lax.all_to_all(slices, OTHER, 0, 0, tiled=True)
    stride_list = [stride for stride in range(-REACH, REACH + 1) if stride != 0]
    ghosts = [passed_along(packets[n], CURVE, stride) for n, stride in enumerate(stride_list)]
    first_ghosts, slices = lax.optimization_barrier((ghosts[:-1], slices))
    ghosts = [*first_ghosts, ghosts[-1]]
    slices = summed_parts(slices, near_devices, "sum_over_z")
    everywhere = lax.all_to_all(slices, NEAR, 0, 0, tiled=True)
    wanted = coarse_list.reshape(1, -1)
    sources = (everywhere, wanted, m2l, group_of, code, l2l)
    lowered = pl.pallas_call(
        down_kernel,
        out_shape=shape((2 * slots, LANES), F32),
        in_specs=[HBM] * len(sources),
        out_specs=VMEM,
        scratch_shapes=[pltpu.VMEM(source.shape, source.dtype) for source in sources]
        + [pltpu.SemaphoreType.DMA((len(sources),))],
        compiler_params=params(24),
        cost_estimate=cost(10**9, 2**23),
        name="down",
    )(*sources)
    sources = (m2l_list, table, *ghosts, m2l, occ, lowered)
    return pl.pallas_call(
        far_kernel,
        out_shape=shape((points, slots), BF16),
        in_specs=[HBM] * len(sources),
        out_specs=VMEM,
        scratch_shapes=[pltpu.VMEM(source.shape, source.dtype) for source in sources]
        + [
            pltpu.VMEM((8 * (slots + 2 * REACH * ghost + 1), LANES), F32),
            pltpu.VMEM((offsets * slots // LANES, LANES), jnp.int32),
            pltpu.VMEM((2 * slots, LANES), F32),
            pltpu.VMEM((2 * slots, LANES), F32),
        ]
        + [pltpu.SMEM((4 * TILE // LANES, LANES), jnp.int32)] * DEPTH
        + [
            pltpu.SemaphoreType.DMA((len(sources),)),
            pltpu.SemaphoreType.DMA((DEPTH,)),
        ],
        compiler_params=params(FAR_MIB),
        cost_estimate=cost(4 * 10**10, 2**24),
        name="far",
    )(*sources)


def solution(mesh):
    along, across = mesh.devices.shape
    rows = 4 if along % 32 == 0 else 1
    torus = Mesh(mesh.devices.reshape(rows, along // rows // 2, 2, across), CURVE + ("oct",))
    boxes = CURVE + ("oct",)
    placed = (
        P(None, boxes),
        P(boxes),
        P(None, boxes),
        P(None, boxes),
        P(boxes),
        P(boxes),
        P(),
        P(),
        P(),
        P(),
        P(),
    )
    return jax.shard_map(
        shards, mesh=torus, in_specs=placed, out_specs=P(None, boxes), check_vma=False
    )
```

```python
import jax
import jax.numpy as jnp
from jax import lax
from jax.experimental import pallas as pl
from jax.experimental.pallas import tpu as pltpu
from jax.sharding import Mesh, PartitionSpec as P

REACH = 3
COARSE = 64
LANES = 128
WIDE = 256
PAD = 8
TILE = 256
DEPTH = 2
PART = 80
FAR_MIB = 60
NEAR = ("y", "oct")
OTHER = ("z", "core")
CURVE = ("y", "z", "core")
NT = (((1,), (1,)), ((), ()))
BF16 = jnp.bfloat16
F32 = jnp.float32

VMEM = pl.BlockSpec(memory_space=pltpu.VMEM)
SMEM = pl.BlockSpec(memory_space=pltpu.SMEM)
HBM = pl.BlockSpec(memory_space=pltpu.HBM)


def params(mib):
    return pltpu.CompilerParams(vmem_limit_bytes=mib * 2**20)


def cost(flops, bytes_accessed):
    return pl.CostEstimate(flops=flops, bytes_accessed=bytes_accessed, transcendentals=0)


def passed_along(block, axis, distance):
    devices = range(lax.axis_size(axis))
    route = [(i - distance, i) for i in devices if i - distance in devices]
    return lax.ppermute(block, axis, route)


def split_rows(columns):
    points, n = columns.shape
    first = columns[:LANES].T
    rest = jnp.concatenate([columns[LANES:], jnp.zeros((WIDE - points, n), F32)], axis=0)
    return first, rest.T


def picked_rows(load, count):
    sublane = lax.broadcasted_iota(jnp.int32, (8, LANES), 0)
    past = [sublane >= 2 * k for k in range(4)]
    for group in range(count // 4):
        merged = load(4 * group, 0)
        for k in range(1, 4):
            merged = jnp.where(past[k], load(4 * group + k, k), merged)
        yield group, merged


def local_kernel(
    leaf_hbm, occ_hbm, rows_hbm, code_hbm, group_hbm, m2m_hbm, up_hbm, table_hbm, partial_ref, *rest
):
    packets = rest[: 2 * REACH]
    table_ref, table_sem, padded, chosen, leaf_ref, occ_ref, rows_ref, code_ref, group_ref, m2m_ref, up_ref, sems = rest[
        2 * REACH :
    ]
    copies = [
        pltpu.make_async_copy(source, target, sems.at[n])
        for n, (source, target) in enumerate(
            [
                (occ_hbm, occ_ref),
                (leaf_hbm, leaf_ref),
                (rows_hbm, rows_ref),
                (code_hbm, code_ref),
                (group_hbm, group_ref),
                (m2m_hbm, m2m_ref),
                (up_hbm, up_ref),
            ]
        )
    ]
    for copy in copies:
        copy.start()
    points, slots = leaf_ref.shape
    parents = code_ref.shape[1]
    ghost = rows_ref.shape[1]
    padded[pl.ds(0, PAD), :] = jnp.zeros((PAD, LANES), F32)
    padded[pl.ds(PAD + 2 * slots, PAD), :] = jnp.zeros((PAD, LANES), F32)
    copies[0].wait()
    copies[1].wait()
    for c in range(0, slots, TILE):
        scale = occ_ref[:, c : c + TILE].astype(F32) * 0.03125
        charged = (leaf_ref[:, c : c + TILE].astype(F32) * scale).astype(BF16).astype(F32)
        first, second = split_rows(charged)
        padded[pl.ds(PAD + 2 * c, TILE, stride=2), :] = first
        padded[pl.ds(PAD + 2 * c + 1, TILE, stride=2), :] = second
        table_ref[pl.ds(c, TILE), :] = first
        table_ref[pl.ds(slots + c, TILE), :] = second
    table_copy = pltpu.make_async_copy(table_ref, table_hbm, table_sem)
    table_copy.start()
    copies[2].wait()

    def one_offset(q, carry):
        base = pl.multiple_of(q * 2 * ghost, 2 * ghost)
        for group, rows in picked_rows(
            lambda n, k: padded[pl.ds(rows_ref[q, n] * 2 + (PAD - 2 * k), 8), :], ghost
        ):
            chosen[pl.ds(base + 8 * group, 8), :] = rows
        return carry

    lax.fori_loop(0, 2 * REACH, one_offset, 0)
    for q in range(2 * REACH):
        first = chosen[pl.ds(q * 2 * ghost, ghost, stride=2), :].T
        second = chosen[pl.ds(q * 2 * ghost + 1, ghost, stride=2), :].T
        packets[q][...] = jnp.concatenate([first, second[: points - LANES]], axis=0).astype(BF16)
    for copy in copies[3:]:
        copy.wait()
    parent = jnp.zeros((points, parents), F32)
    for k in range(8):
        first = table_ref[pl.ds(k, parents, stride=8), :]
        second = table_ref[pl.ds(slots + k, parents, stride=8), :]
        child = jnp.concatenate([first, second], axis=1).astype(BF16)[:, :points]
        parent += lax.dot_general(m2m_ref[k], child, NT, preferred_element_type=F32)
    parent = parent.astype(BF16).astype(F32)
    code = code_ref[...]
    lifted = jnp.zeros((points, parents), F32)
    for k in range(8):
        mine = jnp.where(code == k, parent, 0.0).astype(BF16)
        lifted += jnp.dot(up_ref[k], mine, preferred_element_type=F32)
    high = lifted.astype(BF16)
    low = (lifted - high.astype(F32)).astype(BF16)
    group = lax.broadcasted_iota(jnp.int32, (2 * COARSE, parents), 0)
    left = jnp.where(group == group_ref[...], 1.0, 0.0).astype(BF16)
    right = jnp.where(group - COARSE == group_ref[...], 1.0, 0.0).astype(BF16)

    def summed(member):
        return lax.dot_general(high, member, NT, preferred_element_type=F32) + lax.dot_general(
            low, member, NT, preferred_element_type=F32
        )

    top = PART
    below = jnp.concatenate(
        [summed(right)[top:], jnp.zeros((2 * top - points, 2 * COARSE), F32)], axis=0
    )
    partial_ref[pl.ds(0, top), :] = summed(left)[:top] + below
    partial_ref[pl.ds(top, LANES - top), :] = jnp.zeros((LANES - top, LANES), F32)
    table_copy.wait()


def near_kernel(parts_ref, sum_ref):
    total = jnp.sum(parts_ref[...], axis=0)
    for n in range(sum_ref.shape[0]):
        sum_ref[n] = total


def summed_parts(parts, copies, name):
    return pl.pallas_call(
        near_kernel,
        out_shape=jax.ShapeDtypeStruct((copies,) + parts.shape[1:], F32),
        in_specs=[VMEM],
        out_specs=VMEM,
        compiler_params=params(8),
        cost_estimate=cost(10**6, 2**18),
        name=name,
    )(parts)


def down_kernel(*refs):
    sources, lowered_ref, targets, sems = refs[:6], refs[6], refs[7:13], refs[13]
    coarse_ref, list_ref, m2l_ref, group_ref, code_ref, l2l_ref = targets
    copies = [
        pltpu.make_async_copy(source, target, sems.at[n])
        for n, (source, target) in enumerate(zip(sources, targets))
    ]
    for copy in copies:
        copy.start()
    for copy in copies:
        copy.wait()
    offsets, points, _ = m2l_ref.shape
    parents = code_ref.shape[1]
    coarse = coarse_ref[...].reshape(-1, 2 * COARSE)[:PART].astype(BF16)
    wanted = list_ref[...]
    wanted = jnp.where(wanted == COARSE, 4 * COARSE, wanted)
    row = lax.broadcasted_iota(jnp.int32, (2 * COARSE, wanted.shape[1]), 0)
    left = jnp.where(row == wanted, 1.0, 0.0).astype(BF16)
    right = jnp.where(row - COARSE == wanted, 1.0, 0.0).astype(BF16)
    upper = jnp.dot(coarse, left, preferred_element_type=F32)
    lower = jnp.dot(coarse, right, preferred_element_type=F32)
    partners = jnp.concatenate([upper, lower[: points - PART]], axis=0).astype(BF16)
    sums = [jnp.zeros((points, 2 * COARSE), F32) for _ in range(2)]
    for r in range(offsets):
        at = (r // 2) * 2 * COARSE
        sums[r % 2] += jnp.dot(
            m2l_ref[r], partners[:, at : at + 2 * COARSE], preferred_element_type=F32
        )
    local = (sums[0][:, :COARSE] + sums[1][:, COARSE:]).astype(BF16)
    member = lax.broadcasted_iota(jnp.int32, (COARSE, parents), 0) == group_ref[...]
    pulled = jnp.dot(local, jnp.where(member, 1.0, 0.0).astype(BF16), preferred_element_type=F32)
    code = code_ref[...]
    parent = jnp.zeros((points, parents), F32)
    for k in range(8):
        mine = jnp.where(code == k, pulled, 0.0).astype(BF16)
        parent += jnp.dot(l2l_ref[k], mine, preferred_element_type=F32)
    parent = parent.astype(BF16).astype(F32)
    first, second = split_rows(parent)
    parent_rows = jnp.concatenate([first, second], axis=1).astype(BF16)[:, :points]
    for k in range(8):
        lowered = lax.dot_general(parent_rows, l2l_ref[k], NT, preferred_element_type=F32)
        lowered = jnp.concatenate([lowered, jnp.zeros((parents, WIDE - points), F32)], axis=1)
        lowered_ref[pl.ds(k, parents, stride=8), :] = lowered[:, :LANES]
        lowered_ref[pl.ds(8 * parents + k, parents, stride=8), :] = lowered[:, LANES:]


def parity_split(rows):
    rows = rows.astype(BF16)
    even = lax.rem(lax.broadcasted_iota(jnp.int32, rows.shape, 0), 2) == 0
    zero = jnp.zeros((), BF16)
    return jnp.concatenate([jnp.where(even, rows, zero), jnp.where(even, zero, rows)], axis=1)


def gather_and_translate(accs, windows, window_sems, index, table, m2l_ref, totals):
    points = m2l_ref.shape[1]
    tiles = totals[0].shape[0] // (2 * TILE)
    steps = (m2l_ref.shape[0] // 2) * tiles // 2

    def window_copy(step, slot):
        rows = pl.ds(pl.multiple_of(step * 8, 8), 8)
        return pltpu.make_async_copy(index.at[rows], windows[slot], window_sems.at[slot])

    def load_operators(pair):
        for half in range(2):
            operator = m2l_ref[2 * pair + half].astype(F32)
            operator = jnp.concatenate([operator, jnp.zeros((WIDE - points, points), F32)], axis=0)
            operator = jnp.concatenate([operator, jnp.zeros((WIDE, WIDE - points), F32)], axis=1)
            pltpu.matmul_push_rhs(operator.astype(BF16), 0, half, transpose=True)
            blank = jnp.zeros((2 * TILE, WIDE), BF16)
            pltpu.matmul_acc_lhs(accs[0][half], blank, load_staged_rhs=0)
            totals[1][pl.ds(0, 2 * TILE), :] += pltpu.matmul_pop(accs[0][half])[:, LANES:]

    def gather(slot, which):
        window = windows[slot]

        def load(n, k):
            start = pl.multiple_of(window[4 * which + n // LANES, n % LANES], 8)
            return pltpu.annotate(table, no_bank_conflict=True)[pl.ds(start, 8), :]

        merged = [rows for _, rows in picked_rows(load, 2 * TILE)]
        half = len(merged) // 2
        for n in range(2):
            rows = jnp.concatenate(merged[n * half : (n + 1) * half], axis=0)
            pltpu.matmul_acc_lhs(accs[which][n], parity_split(rows))

    def collect(tile, which):
        rows = pl.ds(pl.multiple_of(lax.rem(tile, tiles) * 2 * TILE, 2 * TILE), 2 * TILE)
        both = pltpu.matmul_pop(accs[which][0]) + pltpu.matmul_pop(accs[which][1])
        totals[0][rows, :] += both[:, :LANES]
        totals[1][rows, :] += both[:, LANES:]

    for slot in range(DEPTH):
        window_copy(slot, slot).start()
    load_operators(0)
    for half in range(2):
        pltpu.matmul_acc_lhs(accs[1][half], jnp.zeros((2 * TILE, WIDE), BF16))

    def some_steps(n, carry):
        for slot in range(DEPTH):
            step = n * DEPTH + slot
            if slot == 0:

                @pl.when((lax.rem(2 * step, tiles) == 0) & (step > 0))
                def _():
                    load_operators(2 * step // tiles)

            window_copy(step, slot).wait()
            gather(slot, 0)
            collect(jnp.maximum(2 * step - 1, 0), 1)
            gather(slot, 1)
            collect(2 * step, 0)
            window_copy(jnp.minimum(step + DEPTH, steps - 1), slot).start()
        return carry

    lax.fori_loop(0, steps // DEPTH, some_steps, 0)
    collect(2 * steps - 1, 1)
    for slot in range(DEPTH):
        window_copy(steps - 1, slot).wait()


def far_kernel(*refs):
    count = 5 + 2 * REACH
    sources, out_ref, targets = refs[:count], refs[count], refs[count + 1 : 2 * count + 1]
    table, index, total_a, total_b, *rest = refs[2 * count + 1 :]
    windows, (sems, window_sems) = rest[:DEPTH], rest[DEPTH:]
    lists, halves, *ghosts = targets[: 2 + 2 * REACH]
    m2l_ref, occ_ref, lowered_ref = targets[2 + 2 * REACH :]
    copies = [
        pltpu.make_async_copy(source, target, sems.at[n])
        for n, (source, target) in enumerate(zip(sources, targets))
    ]
    for copy in copies:
        copy.start()
    offsets, points, _ = m2l_ref.shape
    ghost = ghosts[0].shape[1]
    slots = out_ref.shape[1]
    tiles = slots // TILE

    def spread(first_box, first, second):
        for sublane in range(8):
            at = pl.ds(first_box * 8 + sublane, TILE, stride=8)
            table[at, :] = second if sublane % 2 else first

    total_a[...] = jnp.zeros_like(total_a)
    total_b[...] = jnp.zeros_like(total_b)
    table[pl.ds(8 * (slots + 2 * REACH * ghost), 8), :] = jnp.zeros((8, LANES), F32)
    copies[0].wait()
    blocks = TILE // LANES

    def one_tile(bt, carry):
        for r in range(offsets):
            for j in range(blocks):
                column = pl.multiple_of(bt * TILE + j * LANES, LANES)
                row = (((r // 2) * tiles + bt) * 2 + r % 2) * blocks + j
                index[pl.ds(row, 1), :] = lists[r : r + 1, pl.ds(column, LANES)] * 8
        return carry

    lax.fori_loop(0, tiles, one_tile, 0)
    copies[1].wait()

    def own_tile(n, carry):
        at = pl.multiple_of(n * TILE, TILE)
        spread(at, halves[pl.ds(at, TILE), :], halves[pl.ds(slots + at, TILE), :])
        return carry

    lax.fori_loop(0, tiles, own_tile, 0)
    for q in range(2 * REACH):
        copies[2 + q].wait()
        spread(slots + q * ghost, *split_rows(ghosts[q][...].astype(F32)))
    for copy in copies[2 + 2 * REACH :]:
        copy.wait()
    pl.run_scoped(
        lambda *accs: gather_and_translate(
            (accs[:2], accs[2:]), windows, window_sems, index, table, m2l_ref, (total_a, total_b)
        ),
        *[pltpu.ACC(n % 2)((2 * TILE, WIDE), F32) for n in range(4)],
    )

    def whole(total, at, c):
        even, odd = (total[pl.ds(2 * c + part, TILE, stride=2), :] for part in range(2))
        return (even + odd + lowered_ref[pl.ds(at + c, TILE), :]).T

    for c in range(0, slots, TILE):
        second = whole(total_b, slots, c)[: points - LANES]
        both = jnp.concatenate([whole(total_a, 0, c), second], axis=0)
        live = occ_ref[:, c : c + TILE] > 0
        out_ref[:, c : c + TILE] = jnp.where(live, both, 0.0).astype(BF16)


def shards(
    leaf_mult,
    occupancy,
    ghost_rows,
    m2l_list,
    par_code,
    coarse_of,
    coarse_list,
    m2m,
    coarse_up,
    m2l,
    l2l,
):
    points, slots = leaf_mult.shape
    parents = slots // 8
    offsets = m2l.shape[0]
    ghost = ghost_rows.shape[1]
    shape = jax.ShapeDtypeStruct
    occ = occupancy.reshape(1, slots)
    code = par_code.reshape(1, parents)
    group_of = coarse_of.reshape(1, parents)

    near_devices = lax.axis_size(NEAR)
    table, partial, *packets = pl.pallas_call(
        local_kernel,
        out_shape=[shape((2 * slots, LANES), F32), shape((LANES, 2 * COARSE), F32)]
        + [shape((points, ghost), BF16)] * (2 * REACH),
        in_specs=[HBM] * 7,
        out_specs=[HBM] + [VMEM] * (1 + 2 * REACH),
        scratch_shapes=[
            pltpu.VMEM((2 * slots, LANES), F32),
            pltpu.SemaphoreType.DMA,
            pltpu.VMEM((2 * slots + 2 * PAD, LANES), F32),
            pltpu.VMEM((4 * REACH * ghost, LANES), F32),
            pltpu.VMEM(leaf_mult.shape, BF16),
            pltpu.VMEM(occ.shape, jnp.int32),
            pltpu.SMEM(ghost_rows.shape, jnp.int32),
            pltpu.VMEM(code.shape, jnp.int32),
            pltpu.VMEM(group_of.shape, jnp.int32),
            pltpu.VMEM(m2m.shape, BF16),
            pltpu.VMEM(coarse_up.shape, BF16),
            pltpu.SemaphoreType.DMA((7,)),
        ],
        compiler_params=params(60),
        cost_estimate=cost(10**9, 2**22),
        name="local",
    )(leaf_mult, occ, ghost_rows, code, group_of, m2m, coarse_up)
    slices = partial.reshape(near_devices, LANES // near_devices, 2 * COARSE)
    slices = lax.all_to_all(slices, NEAR, 0, 0, tiled=True)
    slices = summed_parts(slices, lax.axis_size(OTHER), "sum_over_y")
    packets, slices = lax.optimization_barrier((packets, slices))
    slices = lax.all_to_all(slices, OTHER, 0, 0, tiled=True)
    stride_list = [stride for stride in range(-REACH, REACH + 1) if stride != 0]
    ghosts = [passed_along(packets[n], CURVE, stride) for n, stride in enumerate(stride_list)]
    first_ghosts, slices = lax.optimization_barrier((ghosts[:-1], slices))
    ghosts = [*first_ghosts, ghosts[-1]]
    slices = summed_parts(slices, near_devices, "sum_over_z")
    everywhere = lax.all_to_all(slices, NEAR, 0, 0, tiled=True)
    wanted = coarse_list.reshape(1, -1)
    sources = (everywhere, wanted, m2l, group_of, code, l2l)
    lowered = pl.pallas_call(
        down_kernel,
        out_shape=shape((2 * slots, LANES), F32),
        in_specs=[HBM] * len(sources),
        out_specs=VMEM,
        scratch_shapes=[pltpu.VMEM(source.shape, source.dtype) for source in sources]
        + [pltpu.SemaphoreType.DMA((len(sources),))],
        compiler_params=params(24),
        cost_estimate=cost(10**9, 2**23),
        name="down",
    )(*sources)
    sources = (m2l_list, table, *ghosts, m2l, occ, lowered)
    return pl.pallas_call(
        far_kernel,
        out_shape=shape((points, slots), BF16),
        in_specs=[HBM] * len(sources),
        out_specs=VMEM,
        scratch_shapes=[pltpu.VMEM(source.shape, source.dtype) for source in sources]
        + [
            pltpu.VMEM((8 * (slots + 2 * REACH * ghost + 1), LANES), F32),
            pltpu.VMEM((offsets * slots // LANES, LANES), jnp.int32),
            pltpu.VMEM((2 * slots, LANES), F32),
            pltpu.VMEM((2 * slots, LANES), F32),
        ]
        + [pltpu.SMEM((4 * TILE // LANES, LANES), jnp.int32)] * DEPTH
        + [
            pltpu.SemaphoreType.DMA((len(sources),)),
            pltpu.SemaphoreType.DMA((DEPTH,)),
        ],
        compiler_params=params(FAR_MIB),
        cost_estimate=cost(4 * 10**10, 2**24),
        name="far",
    )(*sources)


def solution(mesh):
    along, across = mesh.devices.shape
    rows = 4 if along % 32 == 0 else 1
    torus = Mesh(mesh.devices.reshape(rows, along // rows // 2, 2, across), CURVE + ("oct",))
    boxes = CURVE + ("oct",)
    placed = (
        P(None, boxes),
        P(boxes),
        P(None, boxes),
        P(None, boxes),
        P(boxes),
        P(boxes),
        P(),
        P(),
        P(),
        P(),
        P(),
    )
    return jax.shard_map(
        shards, mesh=torus, in_specs=placed, out_specs=P(None, boxes), check_vma=False
    )
```
